128 devices in a mesh: group: 4 (over x), gy: 4 (over z_lo, core), gx: 8 (over z_hi, y).
Axes of the slice: x: 4, y: 4, z: 4 (z_hi: 2, z_lo: 2; z = z_hi * 2 + z_lo), core: 2. Of those that a mesh axis runs over, the one named last changes fastest.
Arguments:
- east_velocity: float32 [24, 64, 4, 1024], P('group', 'gy', None, 'gx'), may hold values from -6 to 6
- north_velocity: float32 [24, 64, 4, 1024], P('group', 'gy', None, 'gx'), may hold values from -6 to 6
- sea_surface: float32 [64, 4, 1024], P('gy', None, 'gx'), may hold values from -6 to 6
- tracers: float32 [30, 24, 64, 4096], P(None, None, 'gy', ('group', 'gx')), may hold values from -6 to 6
- land_sea: int32 [64, 4096], P('gy', ('group', 'gx')), may hold values 0 or 1
- bottom_level: int32 [64, 4096], P('gy', ('group', 'gx')), may hold values from 1 to 24
- coupling: float32 [30, 30], replicated, may hold values from -1 to 1
Outputs:
- tracers_next: float32 [30, 24, 64, 4096], P(None, None, 'gy', ('group', 'gx'))
- surface_next: float32 [64, 4, 1024], P('gy', None, 'gx')
The draws below stay inside these ranges and needn't reach their ends.
All inputs are finite; a program needn't handle non-finite values. No bound on the sum of `land_sea` on one device may be relied on, other than what follows from the above.
Results may differ from the reference program's by a relative error of at most 0.0003.
Values sent between devices are 32-bit elements; how exact they have to be, the bound alone decides.
A program may use at most 128 MiB of HBM per device.

```python
import jax
import jax.numpy as jnp
from jax import lax

TRACERS = 30
Z = 24
LON_T = 128
NY = 64
NXQ = 1024
NX = 4096
N_GROUP = 4
N_GX = 8


def touch_ends(entries, key, smallest, top_value):
    longest = entries.shape.index(max(entries.shape))
    spots = []
    for shift in (0, 1):
        where = [jax.random.randint(jax.random.fold_in(key, axis), (), 0, length) for axis, length in enumerate(entries.shape)]
        where[longest] = (where[longest] + shift) % entries.shape[longest]
        spots.append(tuple(where))
    return entries.at[spots[0]].set(smallest).at[spots[1]].set(top_value)


def block_levels(stream_key, shape, split, low, top_value):
    def one(position, blocks):
        steps = jax.random.uniform(jax.random.fold_in(jax.random.fold_in(stream_key, 6), position), (blocks,), jnp.float32, low / len(split), top_value / len(split))
        return jnp.repeat(jnp.exp(steps), shape[position] // blocks).reshape((-1,) + (1,) * (len(shape) - position - 1))

    loudness = one(*split[0])
    for cut in split[1:]:
        loudness = loudness * one(*cut)
    return loudness


def noise(own_key, dims, deviation, reach, cuts=(), kind=jnp.bfloat16):
    drawn = jax.random.normal(own_key, dims, jnp.float32) * deviation
    if len(cuts) > 0:
        drawn = block_levels(own_key, dims, cuts, -0.22, 0.18) * drawn
    return jnp.clip(drawn, min=-reach, max=reach).astype(kind)


def setup_inputs(seed: int = 0) -> dict:
    splits = jax.random.split(jax.random.key(seed), 8)
    east_velocity = noise(splits[0], (Z, NY, N_GROUP, NXQ), 1.0, 6.0, ((0, 4), (1, 4), (3, 8)), jnp.float32)
    north_velocity = noise(splits[1], (Z, NY, N_GROUP, NXQ), 1.0, 6.0, ((0, 4), (1, 4), (3, 8)), jnp.float32)
    sea_surface = noise(splits[2], (NY, N_GROUP, NXQ), 1.0, 6.0, ((0, 4), (2, 8)), jnp.float32)
    tracers = noise(splits[3], (TRACERS, Z, NY, NX), 1.0, 6.0, ((2, 4), (3, 32)), jnp.float32)
    land_sea = touch_ends((jax.random.randint(splits[4], (NY, NX), 0, 4) < 3).astype(jnp.int32), jax.random.fold_in(splits[4], 1), 0, 1)
    bottom_level = touch_ends(jax.random.randint(splits[5], (NY, NX), 1, Z + 1), jax.random.fold_in(splits[5], 1), 1, Z).astype(jnp.int32)
    coupling = noise(splits[6], (TRACERS, TRACERS), TRACERS ** -0.5, 1.0, (), jnp.float32)
    return {"east_velocity": east_velocity, "north_velocity": north_velocity, "sea_surface": sea_surface, "tracers": tracers, "land_sea": land_sea, "bottom_level": bottom_level, "coupling": coupling}


CORIOLIS = 0.5
GRAVITY = 0.3
VISCOSITY = 0.1
TIME_STEP = 0.2
BAROTROPIC = 0.5
ADVECTION = 0.15
MIXING = 0.5
KAPPA_BASE = 0.1
KAPPA_SHEAR = 2.0
SHEAR_SCALE = 1.0
ECOLOGY = 0.2


def to_east(field):
    return jnp.roll(field, -1, axis=-1)


def to_west(field):
    return jnp.roll(field, 1, axis=-1)


def to_north(field):
    return jnp.concatenate([field[..., 1:, :], jnp.zeros_like(field[..., :1, :])], axis=-2)


def to_south(field):
    return jnp.concatenate([jnp.zeros_like(field[..., :1, :]), field[..., :-1, :]], axis=-2)


def laplacian(field):
    return to_east(field) + to_west(field) + to_north(field) + to_south(field) - 4.0 * field


def mixing_rate(upper_east, upper_north, lower_east, lower_north):
    shear = (upper_east - lower_east) ** 2 + (upper_north - lower_north) ** 2
    return KAPPA_BASE + KAPPA_SHEAR * shear / (shear + SHEAR_SCALE)


def advect(concentration, east_flow, north_flow, active):
    east_face = active * to_east(active)
    north_face = active * to_north(active)
    flux_east = east_face * (jnp.maximum(east_flow, 0.0) * concentration + jnp.minimum(east_flow, 0.0) * to_east(concentration))
    flux_north = north_face * (jnp.maximum(north_flow, 0.0) * concentration + jnp.minimum(north_flow, 0.0) * to_north(concentration))
    return concentration - ADVECTION * ((flux_east - to_west(flux_east)) + (flux_north - to_south(flux_north)))


def column_step(advected, rates, active, coupling):
    source = jnp.einsum("ts,szyx->tzyx", coupling, jnp.tanh(advected), precision=lax.Precision.HIGHEST)
    forcing = advected + ECOLOGY * active[None] * source
    active_next = jnp.concatenate([active[1:], jnp.zeros_like(active[:1])], axis=0)
    interface = MIXING * rates * active_next
    level_count = advected.shape[1]
    ratio_list = []
    solved_list = []
    ratio_prev = None
    solved_prev = None
    for level in range(level_count):
        above_rate = interface[level]
        if level == 0:
            pivot = 1.0 + above_rate
            solved_now = forcing[:, 0] / pivot
        else:
            below_rate = interface[level - 1]
            pivot = 1.0 + below_rate + above_rate - below_rate * (-ratio_prev)
            solved_now = (forcing[:, level] + below_rate * solved_prev) / pivot
        ratio_now = -above_rate / pivot
        ratio_list.append(ratio_now)
        solved_list.append(solved_now)
        ratio_prev = ratio_now
        solved_prev = solved_now
    result = [None] * level_count
    result[level_count - 1] = solved_list[level_count - 1]
    for level in range(level_count - 2, -1, -1):
        result[level] = solved_list[level] - ratio_list[level] * result[level + 1]
    return jnp.stack(result, axis=1)


def reference(east_velocity, north_velocity, sea_surface, tracers, land_sea, bottom_level, coupling):
    east_flow = east_velocity.reshape(Z, NY, NX)
    north_flow = north_velocity.reshape(Z, NY, NX)
    height = sea_surface.reshape(NY, NX)
    east_next = east_flow + TIME_STEP * (CORIOLIS * north_flow - GRAVITY * (to_east(height) - height) + VISCOSITY * laplacian(east_flow))
    north_next = north_flow + TIME_STEP * (-CORIOLIS * east_flow - GRAVITY * (to_north(height) - height) + VISCOSITY * laplacian(north_flow))
    divergence = jnp.sum(east_flow - to_west(east_flow) + north_flow - to_south(north_flow), axis=0)
    surface_next = (height - (BAROTROPIC / Z) * divergence).reshape(NY, N_GROUP, NXQ)
    below_east = jnp.concatenate([east_next[1:], jnp.zeros_like(east_next[:1])], axis=0)
    below_north = jnp.concatenate([north_next[1:], jnp.zeros_like(north_next[:1])], axis=0)
    rates = mixing_rate(east_next, north_next, below_east, below_north)
    depth = jnp.arange(Z, dtype=jnp.int32)[:, None, None]
    active = ((land_sea[None] > 0) & (depth < bottom_level[None])).astype(jnp.float32)
    advected = lax.map(lambda conc: advect(conc, east_next, north_next, active), tracers)
    block_count = N_GROUP * N_GX

    def one_block(block):
        offset = (block * LON_T).astype(jnp.int32)
        return column_step(
            lax.dynamic_slice_in_dim(advected, offset, LON_T, 3),
            lax.dynamic_slice_in_dim(rates, offset, LON_T, 2),
            lax.dynamic_slice_in_dim(active, offset, LON_T, 2),
            coupling,
        )

    blocks = lax.map(one_block, jnp.arange(block_count, dtype=jnp.int32))
    tracers_next = jnp.moveaxis(blocks, 0, 3).reshape(TRACERS, Z, NY, NX)
    return tracers_next, surface_next
```

```python
import functools

import jax
import jax.numpy as jnp
from jax import lax
from jax.experimental import pallas as pl
from jax.experimental.pallas import tpu as pltpu
from jax.sharding import PartitionSpec as P

CORIOLIS = 0.5
GRAVITY = 0.3
VISCOSITY = 0.1
TIME_STEP = 0.2
BAROTROPIC = 0.5
ADVECTION = 0.15
MIXING = 0.5
KAPPA_BASE = 0.1
KAPPA_SHEAR = 2.0
SHEAR_SCALE = 1.0
ECOLOGY = 0.2

MESH = pl.DeviceIdType.MESH
ANY = pl.BlockSpec(memory_space=pl.ANY)

T = 30
Z = 24
G = 4
L = Z // G
Y = 16
X = 128
PLANES = 2 * L + 1
FOLDED = Y * G
TILE_ROWS = 2 * L * Y
EDGE_ROWS = T * Z + 8
EDGE_COLS = Z * 8 + 8
CHUNKS = 3


def roll(x, by, axis):
    by = by % x.shape[axis]
    return x if by == 0 else pltpu.roll(x, by, axis)


def lanes(shape):
    return lax.broadcasted_iota(jnp.int32, shape, len(shape) - 1)


def rows(shape):
    return lax.broadcasted_iota(jnp.int32, shape, 0)


def exchange_kernel(
    n_gy,
    n_gx,
    u_hbm,
    v_hbm,
    eta_hbm,
    c_hbm,
    land_hbm,
    bottom_hbm,
    coupling_hbm,
    tiles,
    south_rows,
    north_rows,
    west_cols,
    east_cols,
    west_u,
    south_v,
    mix_hi_out,
    mix_lo_out,
    planes,
    conc,
    land,
    bottom,
    coupling,
    edge_q,
    west_q,
    east_q,
    fresh,
    col_pack,
    send_tile,
    send_u,
    send_v,
    row_lo,
    row_hi,
    col_q,
    mix_hi,
    mix_lo,
    load_sem,
    conc_sem,
    send_sem,
    recv_sem,
    tile_send,
    tile_recv,
    u_send,
    u_recv,
    v_send,
    v_recv,
    store_sem,
):
    g = lax.axis_index("group")
    j = lax.axis_index("gy")
    i = lax.axis_index("gx")
    i_east = lax.rem(i + 1, n_gx)
    i_west = lax.rem(i + n_gx - 1, n_gx)
    has_south = j > 0
    has_north = j < n_gy - 1

    loads = [
        pltpu.make_async_copy(u_hbm, planes.at[pl.ds(0, L), pl.ds(8, FOLDED)], load_sem.at[0]),
        pltpu.make_async_copy(v_hbm, planes.at[pl.ds(L, L), pl.ds(8, FOLDED)], load_sem.at[1]),
        pltpu.make_async_copy(eta_hbm, planes.at[2 * L, pl.ds(8, FOLDED)], load_sem.at[2]),
        pltpu.make_async_copy(land_hbm, land, load_sem.at[3]),
        pltpu.make_async_copy(bottom_hbm, bottom, load_sem.at[4]),
        pltpu.make_async_copy(coupling_hbm, coupling, load_sem.at[5]),
    ]
    for load in loads:
        load.start()
    part_rows = T * Z * Y // CHUNKS
    conc_loads = [
        pltpu.make_async_copy(
            c_hbm.at[pl.ds(n * part_rows, part_rows)],
            conc.at[pl.ds(n * part_rows, part_rows)],
            conc_sem.at[n],
        )
        for n in range(CHUNKS)
    ]
    for load in conc_loads:
        load.start()

    barrier = pltpu.get_barrier_semaphore()
    for d in range(1, G):
        pl.semaphore_signal(barrier, inc=1, device_id=(lax.rem(g + d, G), j, i), device_id_type=MESH)
    for d in range(G):
        pl.semaphore_signal(barrier, inc=1, device_id=(d, j, i_east), device_id_type=MESH)
        pl.semaphore_signal(barrier, inc=1, device_id=(d, j, i_west), device_id_type=MESH)

    @pl.when(has_south)
    def _():
        for d in range(G):
            pl.semaphore_signal(barrier, inc=1, device_id=(d, j - 1, i), device_id_type=MESH)

    @pl.when(has_north)
    def _():
        for d in range(G):
            pl.semaphore_signal(barrier, inc=1, device_id=(d, j + 1, i), device_id_type=MESH)

    for load in loads:
        load.wait()
    lane = lanes((FOLDED, X))
    packed = jnp.zeros((FOLDED, X), jnp.float32)
    for p in range(PLANES):
        packed = jnp.where(lane // 2 == p, roll(planes[p, 8 : 8 + FOLDED, :], 2 * p + 1, 1), packed)
    edge_q[...] = packed

    around = lax.div(j + n_gy - 1, n_gy) + lax.div(2 * (n_gy - 1) - j, n_gy)
    pl.semaphore_wait(barrier, G - 1 + 2 * G + G * around)

    def remote(src, dst, n, device):
        return pltpu.make_async_remote_copy(
            src_ref=src,
            dst_ref=dst,
            send_sem=send_sem.at[n],
            recv_sem=recv_sem.at[n],
            device_id=device,
            device_id_type=MESH,
        )

    to_north = remote(planes.at[:, pl.ds(FOLDED, 8)], planes.at[:, pl.ds(0, 8)], 0, (g, j + 1, i))
    to_south = remote(
        planes.at[:, pl.ds(8, 8)], planes.at[:, pl.ds(8 + FOLDED, 8)], 1, (g, j - 1, i)
    )
    to_east = remote(edge_q, west_q, 2, (g, j, i_east))
    to_west = remote(edge_q, east_q, 3, (g, j, i_west))
    to_east.start()
    to_west.start()

    @pl.when(has_north)
    def _():
        to_north.start()

    @pl.when(has_south)
    def _():
        to_south.start()

    depth = jnp.where(land[...] > 0, bottom[...], 0).astype(jnp.float32)
    row_lo[pl.ds(T * Z, 8), :] = jnp.broadcast_to(depth[0:1], (8, X))
    row_hi[pl.ds(T * Z, 8), :] = jnp.broadcast_to(depth[Y - 1 : Y], (8, X))
    for n in range(CHUNKS):
        conc_loads[n].wait()

        def take_rows(t, carry):
            base = pl.multiple_of(t * (Z * Y), Z * Y)
            place = pl.multiple_of(t * Z, 8)
            row_lo[pl.ds(place, Z), :] = conc[pl.ds(base, Z, stride=Y), :]
            row_hi[pl.ds(place, Z), :] = conc[pl.ds(base + Y - 1, Z, stride=Y), :]
            return carry

        lax.fori_loop(n * (T // CHUNKS), (n + 1) * (T // CHUNKS), take_rows, 0)

    rows_north = remote(row_hi, south_rows, 4, (g, j + 1, i))
    rows_south = remote(row_lo, north_rows, 5, (g, j - 1, i))

    @pl.when(has_north)
    def _():
        rows_north.start()

    @pl.when(has_south)
    def _():
        rows_south.start()

    @pl.when(has_south)
    def _():
        to_north.wait_recv()

    @pl.when(has_north)
    def _():
        to_south.wait_recv()

    @pl.when(jnp.logical_not(has_south))
    def _():
        planes[:, pl.ds(0, 8), :] = jnp.zeros((PLANES, 8, X), jnp.float32)

    @pl.when(jnp.logical_not(has_north))
    def _():
        planes[:, pl.ds(8 + FOLDED, 8), :] = jnp.zeros((PLANES, 8, X), jnp.float32)

    to_east.wait_recv()
    to_west.wait_recv()
    fold = lax.rem(rows((FOLDED, X)), G)
    qw = west_q[...]
    qe = east_q[...]
    qw_turned = jnp.where(fold == 0, roll(qw, -(G - 1), 0), roll(qw, 1, 0))
    qe_turned = jnp.where(fold == G - 1, roll(qe, G - 1, 0), roll(qe, -1, 0))
    qw = jnp.where(i == 0, qw_turned, qw)
    qe = jnp.where(i == n_gx - 1, qe_turned, qe)
    west_q[...] = jnp.where(lane % 2 == 1, roll(qw, 1, 1), roll(qe, -1, 1))

    def eastern(x, edge):
        return jnp.where(lane == X - 1, edge, roll(x, -1, 1))

    def western(x, edge):
        return jnp.where(lane == 0, edge, roll(x, 1, 1))

    def sides(p):
        return roll(west_q[...], -(2 * p + 1), 1)

    def at(p, shift):
        return planes[p, 8 + shift : 8 + shift + FOLDED, :]

    height = at(2 * L, 0)
    push_east = GRAVITY * (eastern(height, sides(2 * L)) - height)
    push_north = GRAVITY * (at(2 * L, G) - height)
    spread = jnp.zeros((FOLDED, X), jnp.float32)
    pack = jnp.zeros((FOLDED, X), jnp.float32)
    for k in range(L):
        u = at(k, 0)
        v = at(L + k, 0)
        u_side = sides(k)
        v_side = sides(L + k)
        u_west = western(u, u_side)
        v_south = at(L + k, -G)
        lap_u = eastern(u, u_side) + u_west + at(k, G) + at(k, -G) - 4.0 * u
        lap_v = eastern(v, v_side) + western(v, v_side) + at(L + k, G) + v_south - 4.0 * v
        u_new = u + TIME_STEP * (CORIOLIS * v - push_east + VISCOSITY * lap_u)
        v_new = v + TIME_STEP * (-CORIOLIS * u - push_north + VISCOSITY * lap_v)
        spread = spread + (u - u_west + v - v_south)
        fresh[pl.ds(k * FOLDED, FOLDED), :] = u_new
        fresh[pl.ds((L + k) * FOLDED, FOLDED), :] = v_new
        pack = jnp.where(lane == k, roll(u_new, k + 1, 1), pack)
    col_pack[...] = pack
    for f in range(G):
        for p in range(2 * L):
            send_tile[f, pl.ds(p * Y, Y), :] = fresh[pl.ds(p * FOLDED + f, Y, stride=G), :]
        send_tile[f, pl.ds(TILE_ROWS, FOLDED), :] = spread
        send_u[f] = col_pack[pl.ds(f, Y, stride=G), :]
        send_v[f] = jnp.zeros((8, X), jnp.float32)
        send_v[f, pl.ds(0, L), :] = fresh[
            pl.ds(L * FOLDED + (Y - 1) * G + f, L, stride=FOLDED), :
        ]

    def tile_copy(d):
        other = lax.rem(g + d, G)
        return pltpu.make_async_remote_copy(
            src_ref=send_tile.at[other],
            dst_ref=tiles.at[g],
            send_sem=tile_send.at[other],
            recv_sem=tile_recv.at[g],
            device_id=(other, j, i),
            device_id_type=MESH,
        )

    def u_copy(f):
        crossed = jnp.where(i == n_gx - 1, 1, 0)
        return pltpu.make_async_remote_copy(
            src_ref=send_u.at[f],
            dst_ref=west_u.at[g],
            send_sem=u_send.at[f],
            recv_sem=u_recv.at[g],
            device_id=(lax.rem(f + crossed, G), j, i_east),
            device_id_type=MESH,
        )

    def v_copy(f):
        return pltpu.make_async_remote_copy(
            src_ref=send_v.at[f],
            dst_ref=south_v.at[g],
            send_sem=v_send.at[f],
            recv_sem=v_recv.at[g],
            device_id=(f, j + 1, i),
            device_id_type=MESH,
        )

    for d in (2, 1, 3):
        tile_copy(d).start()
    for f in range(G):
        u_copy(f).start()

    @pl.when(has_north)
    def _():
        for f in range(G):
            v_copy(f).start()

    own_tile = pltpu.make_async_copy(send_tile.at[g], tiles.at[g], store_sem.at[0])
    own_tile.start()

    small = lanes((8, X))

    def take_cols(z, carry):
        parts = [jnp.zeros((8, X), jnp.float32) for _ in range(4)]
        for t in range(T):
            for o in range(2):
                base = pl.multiple_of(t * (Z * Y) + z * Y + 8 * o, 8)
                n = (2 * t + o) % 4
                parts[n] = jnp.where(
                    small // 2 == 32 * o + t,
                    roll(conc[pl.ds(base, 8), :], 64 * o + 2 * t + 1, 1),
                    parts[n],
                )
        col_q[pl.ds(pl.multiple_of(z * 8, 8), 8), :] = (parts[0] + parts[1]) + (
            parts[2] + parts[3]
        )
        return carry

    lax.fori_loop(0, Z, take_cols, 0)
    col_q[pl.ds(Z * 8, 8), :] = jnp.where(
        small // 2 == 0,
        roll(depth[0:8], 1, 1),
        jnp.where(small // 2 == 32, roll(depth[8:16], 65, 1), 0.0),
    )
    up = jnp.where(i == n_gx - 1, 1, 0)
    down = jnp.where(i == 0, G - 1, 0)
    cols_east = remote(col_q, west_cols, 6, (lax.rem(g + up, G), j, i_east))
    cols_west = remote(col_q, east_cols, 7, (lax.rem(g + down, G), j, i_west))
    cols_east.start()
    cols_west.start()

    tall = (rows((8 * T, T)) // 8 == lanes((8 * T, T))).astype(jnp.bfloat16)
    wide = (rows((T, 8 * T)) == lanes((T, 8 * T)) // 8).astype(jnp.bfloat16)
    own = lax.rem(rows((8 * T, 8 * T)), 8) == lax.rem(lanes((8 * T, 8 * T)), 8)
    hi = coupling[...].astype(jnp.bfloat16)
    lo = (coupling[...] - hi.astype(jnp.float32)).astype(jnp.bfloat16)
    for part, place in ((hi, mix_hi), (lo, mix_lo)):
        half = jnp.dot(tall, part, preferred_element_type=jnp.float32).astype(jnp.bfloat16)
        whole = jnp.dot(half, wide, preferred_element_type=jnp.float32)
        place[...] = jnp.where(own, whole, 0.0).astype(jnp.bfloat16)
    stores = [
        pltpu.make_async_copy(mix_hi, mix_hi_out, store_sem.at[1]),
        pltpu.make_async_copy(mix_lo, mix_lo_out, store_sem.at[2]),
    ]
    for store in stores:
        store.start()

    for d in range(1, G):
        other = lax.rem(g + d, G)
        pltpu.make_async_remote_copy(
            src_ref=send_tile.at[other],
            dst_ref=tiles.at[other],
            send_sem=tile_send.at[other],
            recv_sem=tile_recv.at[other],
            device_id=(other, j, i),
            device_id_type=MESH,
        ).wait()
    for f in range(G):
        pltpu.make_async_remote_copy(
            src_ref=send_u.at[f],
            dst_ref=west_u.at[f],
            send_sem=u_send.at[f],
            recv_sem=u_recv.at[f],
            device_id=(f, j, i_east),
            device_id_type=MESH,
        ).wait()

    @pl.when(has_north)
    def _():
        to_north.wait_send()
        rows_north.wait_send()
        rows_south.wait_recv()
        for f in range(G):
            v_copy(f).wait_send()

    @pl.when(has_south)
    def _():
        to_south.wait_send()
        rows_south.wait_send()
        rows_north.wait_recv()
        for f in range(G):
            pltpu.make_async_remote_copy(
                src_ref=send_v.at[f],
                dst_ref=south_v.at[f],
                send_sem=v_send.at[f],
                recv_sem=v_recv.at[f],
                device_id=(f, j - 1, i),
                device_id_type=MESH,
            ).wait_recv()

    to_east.wait_send()
    to_west.wait_send()
    cols_east.wait()
    cols_west.wait()
    own_tile.wait()
    for store in stores:
        store.wait()


def exchange(n_gy, n_gx, u, v, eta, conc, land, bottom, coupling):
    f32 = jnp.float32
    dma = pltpu.SemaphoreType.DMA
    out_shape = (
        jax.ShapeDtypeStruct((G, TILE_ROWS + FOLDED, X), f32),
        jax.ShapeDtypeStruct((EDGE_ROWS, X), f32),
        jax.ShapeDtypeStruct((EDGE_ROWS, X), f32),
        jax.ShapeDtypeStruct((EDGE_COLS, X), f32),
        jax.ShapeDtypeStruct((EDGE_COLS, X), f32),
        jax.ShapeDtypeStruct((G, Y, X), f32),
        jax.ShapeDtypeStruct((G, 8, X), f32),
        jax.ShapeDtypeStruct((8 * T, 8 * T), jnp.bfloat16),
        jax.ShapeDtypeStruct((8 * T, 8 * T), jnp.bfloat16),
    )
    return pl.pallas_call(
        functools.partial(exchange_kernel, n_gy, n_gx),
        out_shape=out_shape,
        in_specs=[ANY] * 7,
        out_specs=(ANY,) * 9,
        scratch_shapes=[
            pltpu.VMEM((PLANES, FOLDED + 16, X), f32),
            pltpu.VMEM((T * Z * Y, X), f32),
            pltpu.VMEM((Y, X), jnp.int32),
            pltpu.VMEM((Y, X), jnp.int32),
            pltpu.VMEM((T, T), f32),
            pltpu.VMEM((FOLDED, X), f32),
            pltpu.VMEM((FOLDED, X), f32),
            pltpu.VMEM((FOLDED, X), f32),
            pltpu.VMEM((2 * L * FOLDED, X), f32),
            pltpu.VMEM((FOLDED, X), f32),
            pltpu.VMEM((G, TILE_ROWS + FOLDED, X), f32),
            pltpu.VMEM((G, Y, X), f32),
            pltpu.VMEM((G, 8, X), f32),
            pltpu.VMEM((EDGE_ROWS, X), f32),
            pltpu.VMEM((EDGE_ROWS, X), f32),
            pltpu.VMEM((EDGE_COLS, X), f32),
            pltpu.VMEM((8 * T, 8 * T), jnp.bfloat16),
            pltpu.VMEM((8 * T, 8 * T), jnp.bfloat16),
            dma((6,)),
            dma((CHUNKS,)),
            dma((8,)),
            dma((8,)),
            dma((G,)),
            dma((G,)),
            dma((G,)),
            dma((G,)),
            dma((G,)),
            dma((G,)),
            dma((3,)),
        ],
        compiler_params=pltpu.CompilerParams(
            collective_id=0, has_side_effects=True, vmem_limit_bytes=32 * 1024 * 1024
        ),
        name="exchange",
    )(u, v, eta, conc, land, bottom, coupling)


Z_PART = 4
T_PART = 5
COEF = 9


def column_kernel(
    n_gy,
    c_hbm,
    tiles_hbm,
    south_rows_hbm,
    north_rows_hbm,
    west_cols_hbm,
    east_cols_hbm,
    west_u_hbm,
    south_v_hbm,
    mix_hi_hbm,
    mix_lo_hbm,
    eta_hbm,
    land_hbm,
    bottom_hbm,
    out_hbm,
    surface_hbm,
    conc,
    solved,
    coef,
    tiles,
    south_rows,
    north_rows,
    west_cols,
    east_cols,
    west_u,
    south_v,
    mix_hi,
    mix_lo,
    eta,
    land,
    bottom,
    surface,
    adv_a,
    adv_b,
    hi_a,
    lo_a,
    hi_b,
    lo_b,
    load_sem,
    conc_sem,
    out_sem,
):
    j = lax.axis_index("gy")
    pairs = (
        (land_hbm, land),
        (bottom_hbm, bottom),
        (tiles_hbm, tiles),
        (west_u_hbm, west_u),
        (south_v_hbm, south_v),
        (west_cols_hbm, west_cols),
        (east_cols_hbm, east_cols),
        (south_rows_hbm, south_rows),
        (north_rows_hbm, north_rows),
        (eta_hbm, eta),
        (mix_hi_hbm, mix_hi),
        (mix_lo_hbm, mix_lo),
    )
    loads = [pltpu.make_async_copy(a, b, load_sem.at[n]) for n, (a, b) in enumerate(pairs)]
    for load in loads:
        load.start()
    conc_loads = [
        pltpu.make_async_copy(
            c_hbm.at[:, pl.ds(n * Z_PART, Z_PART)],
            conc.at[:, pl.ds(n * Z_PART, Z_PART), pl.ds(8, Y)],
            conc_sem.at[n],
        )
        for n in range(Z // Z_PART)
    ]
    for load in conc_loads:
        load.start()
    for load in loads:
        load.wait()

    flat = conc.reshape(T * Z * 32, X)
    south_ok = j > 0
    north_ok = j < n_gy - 1

    def put_rows(t, carry):
        place = pl.multiple_of(t * Z, 8)
        base = pl.multiple_of(t * (Z * 32), 8)
        flat[pl.ds(base + 7, Z, stride=32), :] = jnp.where(
            south_ok, south_rows[pl.ds(place, Z), :], 0.0
        )
        flat[pl.ds(base + 8 + Y, Z, stride=32), :] = jnp.where(
            north_ok, north_rows[pl.ds(place, Z), :], 0.0
        )
        return carry

    lax.fori_loop(0, T, put_rows, 0)

    lane = lanes((8, X))
    odd = lane % 2 == 1

    def put_cols(z, carry):
        place = pl.ds(pl.multiple_of(z * 8, 8), 8)
        west_cols[place, :] = jnp.where(
            odd, roll(west_cols[place, :], 1, 1), roll(east_cols[place, :], -1, 1)
        )
        return carry

    lax.fori_loop(0, Z + 1, put_cols, 0)

    total = tiles[0, pl.ds(TILE_ROWS, FOLDED), :]
    for m in range(1, G):
        total = total + tiles[m, pl.ds(TILE_ROWS, FOLDED), :]
    surface[...] = eta[...] - (BAROTROPIC / Z) * total
    surface_store = pltpu.make_async_copy(surface, surface_hbm, out_sem.at[T // T_PART])
    surface_store.start()

    wide = lanes((Y, X))
    tall = rows((Y, X))
    depth = jnp.where(land[...] > 0, bottom[...], 0).astype(jnp.float32)
    depth_side = west_cols[pl.ds(Z * 8, 8), :]
    depth_side = jnp.concatenate([roll(depth_side, -1, 1), roll(depth_side, -65, 1)], axis=0)
    depth_east = jnp.where(wide == X - 1, depth_side, roll(depth, -1, 1))
    depth_west = jnp.where(wide == 0, depth_side, roll(depth, 1, 1))
    above = jnp.where(north_ok, north_rows[pl.ds(T * Z, 8), :], 0.0)
    below = jnp.where(south_ok, south_rows[pl.ds(T * Z, 8), :], 0.0)
    depth_north = jnp.where(
        tall == Y - 1, jnp.concatenate([above, above], axis=0), roll(depth, -1, 0)
    )
    depth_south = jnp.where(tall == 0, jnp.concatenate([below, below], axis=0), roll(depth, 1, 0))
    reach_east = jnp.minimum(depth, depth_east)
    reach_west = jnp.minimum(depth, depth_west)
    reach_north = jnp.minimum(depth, depth_north)
    reach_south = jnp.minimum(depth, depth_south)

    def flows(z):
        m, k = z // L, z % L
        return tiles[m, pl.ds(k * Y, Y), :], tiles[m, pl.ds((L + k) * Y, Y), :]

    g_above = jnp.zeros((Y, X), jnp.float32)
    r_above = jnp.zeros((Y, X), jnp.float32)
    u, v = flows(0)
    for z in range(Z):
        m, k = z // L, z % L
        u_west = jnp.where(wide == 0, roll(west_u[m], -k, 1), roll(u, 1, 1))
        row = jnp.where(south_ok, south_v[m, k : k + 1, :], 0.0)
        v_south = jnp.where(tall == 0, jnp.broadcast_to(row, (Y, X)), roll(v, 1, 0))
        ke = jnp.where(reach_east > z, ADVECTION, 0.0)
        kw = jnp.where(reach_west > z, ADVECTION, 0.0)
        kn = jnp.where(reach_north > z, ADVECTION, 0.0)
        ks = jnp.where(reach_south > z, ADVECTION, 0.0)
        coef[z, 0] = (
            1.0
            - ke * jnp.maximum(u, 0.0)
            + kw * jnp.minimum(u_west, 0.0)
            - kn * jnp.maximum(v, 0.0)
            + ks * jnp.minimum(v_south, 0.0)
        )
        coef[z, 1] = -ke * jnp.minimum(u, 0.0)
        coef[z, 2] = kw * jnp.maximum(u_west, 0.0)
        coef[z, 3] = -kn * jnp.minimum(v, 0.0)
        coef[z, 4] = ks * jnp.maximum(v_south, 0.0)
        if z < Z - 1:
            u_next, v_next = flows(z + 1)
            shear = (u - u_next) ** 2 + (v - v_next) ** 2
            rate = KAPPA_BASE + KAPPA_SHEAR * shear / (shear + SHEAR_SCALE)
            g = jnp.where(depth > z + 1, MIXING * rate, 0.0)
            u, v = u_next, v_next
        else:
            g = jnp.zeros((Y, X), jnp.float32)
        inverse = 1.0 / (1.0 + g_above + g - g_above * r_above)
        coef[z, 5] = inverse
        coef[z, 6] = jnp.where(depth > z, ECOLOGY * inverse, 0.0)
        coef[z, 7] = g_above * inverse
        r_above = g * inverse
        coef[z, 8] = r_above
        g_above = g

    def zero_top(t, carry):
        solved[t, 0] = jnp.zeros((Y, X), jnp.float32)
        return carry

    lax.fori_loop(0, T, zero_top, 0)

    def advance(z, adv, hi_ref, lo_ref):
        side = west_cols[pl.ds(pl.multiple_of(z * 8, 8), 8), :]
        for o in range(2):
            ks = [coef[z, n, 8 * o : 8 * o + 8, :] for n in range(5)]
            for pair in range(T // 2):
                both = []
                for t in (2 * pair, 2 * pair + 1):
                    c = conc[t, z, 8 + 8 * o : 16 + 8 * o, :]
                    edge = roll(side, -(64 * o + 2 * t + 1), 1)
                    east = jnp.where(lane == X - 1, edge, roll(c, -1, 1))
                    west = jnp.where(lane == 0, edge, roll(c, 1, 1))
                    north = conc[t, z, 9 + 8 * o : 17 + 8 * o, :]
                    south = conc[t, z, 7 + 8 * o : 15 + 8 * o, :]
                    a = (ks[0] * c + ks[1] * east) + (
                        ks[2] * west + (ks[3] * north + ks[4] * south)
                    )
                    adv[t, 8 * o : 8 * o + 8, :] = a
                    both.append(jnp.tanh(a))
                y = jnp.concatenate(both, axis=0)
                hi = y.astype(jnp.bfloat16)
                lo = (y - hi.astype(jnp.float32)).astype(jnp.bfloat16)
                hi_ref[16 * pair : 16 * pair + 16, o * X : o * X + X] = hi
                lo_ref[16 * pair : 16 * pair + 16, o * X : o * X + X] = lo

    def mix(hi_ref, lo_ref):
        return (
            jnp.dot(mix_hi[...], hi_ref[...], preferred_element_type=jnp.float32)
            + jnp.dot(mix_lo[...], hi_ref[...], preferred_element_type=jnp.float32)
            + jnp.dot(mix_hi[...], lo_ref[...], preferred_element_type=jnp.float32)
        )

    def finish(z, adv, source):
        for o in range(2):
            ks = [coef[z, n, 8 * o : 8 * o + 8, :] for n in range(5, 8)]
            for t in range(T):
                s = source[8 * t : 8 * t + 8, o * X : o * X + X]
                solved[t, z + 1, 8 * o : 8 * o + 8, :] = (
                    ks[0] * adv[t, 8 * o : 8 * o + 8, :]
                    + ks[1] * s
                    + ks[2] * solved[t, z, 8 * o : 8 * o + 8, :]
                )

    def two(i, carry):
        z = 2 * i

        source = mix(hi_a, lo_a)
        advance(z + 1, adv_b, hi_b, lo_b)
        finish(z, adv_a, source)
        source = mix(hi_b, lo_b)
        advance(z + 2, adv_a, hi_a, lo_a)
        finish(z + 1, adv_b, source)
        return carry

    for load in conc_loads:
        load.wait()
    advance(0, adv_a, hi_a, lo_a)
    lax.fori_loop(0, Z // 2 - 1, two, 0)
    source = mix(hi_a, lo_a)
    advance(Z - 1, adv_b, hi_b, lo_b)
    finish(Z - 2, adv_a, source)
    finish(Z - 1, adv_b, mix(hi_b, lo_b))

    def store(n):
        return pltpu.make_async_copy(
            solved.at[pl.ds(n * T_PART, T_PART), pl.ds(1, Z)],
            out_hbm.at[pl.ds(n * T_PART, T_PART)],
            out_sem.at[n],
        )

    def back(n, carry):
        base = n * T_PART
        x = [solved[base + t, Z] for t in range(T_PART)]
        for z in range(Z - 2, -1, -1):
            r = coef[z, 8]
            for t in range(T_PART):
                x[t] = solved[base + t, z + 1] + r * x[t]
                solved[base + t, z + 1] = x[t]
        store(n).start()
        return carry

    lax.fori_loop(0, T // T_PART, back, 0)
    for n in range(T // T_PART):
        store(n).wait()
    surface_store.wait()


def columns(n_gy, conc, parts, eta, land, bottom):
    f32 = jnp.float32
    dma = pltpu.SemaphoreType.DMA
    mix_type = pltpu.VMEM((8 * T, 2 * X), jnp.bfloat16)
    return pl.pallas_call(
        functools.partial(column_kernel, n_gy),
        out_shape=(
            jax.ShapeDtypeStruct((T, Z, Y, X), f32),
            jax.ShapeDtypeStruct((FOLDED, X), f32),
        ),
        in_specs=[ANY] * 13,
        out_specs=(ANY, ANY),
        scratch_shapes=[
            pltpu.VMEM((T, Z, 32, X), f32),
            pltpu.VMEM((T, Z + 1, Y, X), f32),
            pltpu.VMEM((Z, COEF, Y, X), f32),
            pltpu.VMEM((G, TILE_ROWS + FOLDED, X), f32),
            pltpu.VMEM((EDGE_ROWS, X), f32),
            pltpu.VMEM((EDGE_ROWS, X), f32),
            pltpu.VMEM((EDGE_COLS, X), f32),
            pltpu.VMEM((EDGE_COLS, X), f32),
            pltpu.VMEM((G, Y, X), f32),
            pltpu.VMEM((G, 8, X), f32),
            pltpu.VMEM((8 * T, 8 * T), jnp.bfloat16),
            pltpu.VMEM((8 * T, 8 * T), jnp.bfloat16),
            pltpu.VMEM((FOLDED, X), f32),
            pltpu.VMEM((Y, X), jnp.int32),
            pltpu.VMEM((Y, X), jnp.int32),
            pltpu.VMEM((FOLDED, X), f32),
            pltpu.VMEM((T, Y, X), f32),
            pltpu.VMEM((T, Y, X), f32),
            mix_type,
            mix_type,
            mix_type,
            mix_type,
            dma((12,)),
            dma((Z // Z_PART,)),
            dma((T // T_PART + 1,)),
        ],
        compiler_params=pltpu.CompilerParams(vmem_limit_bytes=48 * 1024 * 1024),
        name="columns",
    )(conc, *parts, eta, land, bottom)


def shards(east_velocity, north_velocity, sea_surface, tracers, land_sea, bottom_level, coupling):
    n_gy = lax.axis_size("gy")
    n_gx = lax.axis_size("gx")
    eta = sea_surface.reshape(FOLDED, X)
    parts = exchange(
        n_gy,
        n_gx,
        east_velocity.reshape(L, FOLDED, X),
        north_velocity.reshape(L, FOLDED, X),
        eta,
        tracers.reshape(T * Z * Y, X),
        land_sea,
        bottom_level,
        coupling,
    )
    tracers_next, surface_next = columns(n_gy, tracers, parts, eta, land_sea, bottom_level)
    return tracers_next, surface_next.reshape(Y, G, X)


def solution(mesh):
    placed = (
        P("group", "gy", None, "gx"),
        P("group", "gy", None, "gx"),
        P("gy", None, "gx"),
        P(None, None, "gy", ("group", "gx")),
        P("gy", ("group", "gx")),
        P("gy", ("group", "gx")),
        P(),
    )
    return jax.shard_map(
        shards,
        mesh=mesh,
        in_specs=placed,
        out_specs=(P(None, None, "gy", ("group", "gx")), P("gy", None, "gx")),
        check_vma=False,
    )
```

```python
import functools

import jax
import jax.numpy as jnp
from jax import lax
from jax.experimental import pallas as pl
from jax.experimental.pallas import tpu as pltpu
from jax.sharding import PartitionSpec as P

CORIOLIS = 0.5
GRAVITY = 0.3
VISCOSITY = 0.1
TIME_STEP = 0.2
BAROTROPIC = 0.5
ADVECTION = 0.15
MIXING = 0.5
KAPPA_BASE = 0.1
KAPPA_SHEAR = 2.0
SHEAR_SCALE = 1.0
ECOLOGY = 0.2

MESH = pl.DeviceIdType.MESH
HBM = pl.BlockSpec(memory_space=pltpu.HBM)

T = 30
Z = 24
G = 4
L = Z // G
Y = 16
X = 128
PLANES = 2 * L + 1
FOLDED = Y * G
TILE_ROWS = 2 * L * Y
EDGE_ROWS = T * Z + 8
EDGE_COLS = Z * 8 + 8
CHUNKS = 3


def roll(x, by, axis):
    by = by % x.shape[axis]
    return x if by == 0 else pltpu.roll(x, by, axis)


def lanes(shape):
    return lax.broadcasted_iota(jnp.int32, shape, len(shape) - 1)


def rows(shape):
    return lax.broadcasted_iota(jnp.int32, shape, 0)


def exchange_kernel(
    n_gy,
    n_gx,
    u_hbm,
    v_hbm,
    eta_hbm,
    c_hbm,
    land_hbm,
    bottom_hbm,
    coupling_hbm,
    tiles,
    south_rows,
    north_rows,
    west_cols,
    east_cols,
    west_u,
    south_v,
    mix_hi_out,
    mix_lo_out,
    planes,
    conc,
    land,
    bottom,
    coupling,
    edge_q,
    west_q,
    east_q,
    fresh,
    col_pack,
    send_tile,
    send_u,
    send_v,
    row_lo,
    row_hi,
    col_q,
    mix_hi,
    mix_lo,
    load_sem,
    conc_sem,
    send_sem,
    recv_sem,
    tile_send,
    tile_recv,
    u_send,
    u_recv,
    v_send,
    v_recv,
    store_sem,
):
    g = lax.axis_index("group")
    j = lax.axis_index("gy")
    i = lax.axis_index("gx")
    i_east = lax.rem(i + 1, n_gx)
    i_west = lax.rem(i + n_gx - 1, n_gx)
    has_south = j > 0
    has_north = j < n_gy - 1

    loads = [
        pltpu.make_async_copy(u_hbm, planes.at[pl.ds(0, L), pl.ds(8, FOLDED)], load_sem.at[0]),
        pltpu.make_async_copy(v_hbm, planes.at[pl.ds(L, L), pl.ds(8, FOLDED)], load_sem.at[1]),
        pltpu.make_async_copy(eta_hbm, planes.at[2 * L, pl.ds(8, FOLDED)], load_sem.at[2]),
        pltpu.make_async_copy(land_hbm, land, load_sem.at[3]),
        pltpu.make_async_copy(bottom_hbm, bottom, load_sem.at[4]),
        pltpu.make_async_copy(coupling_hbm, coupling, load_sem.at[5]),
    ]
    for load in loads:
        load.start()
    part_rows = T * Z * Y // CHUNKS
    conc_loads = [
        pltpu.make_async_copy(
            c_hbm.at[pl.ds(n * part_rows, part_rows)],
            conc.at[pl.ds(n * part_rows, part_rows)],
            conc_sem.at[n],
        )
        for n in range(CHUNKS)
    ]
    for load in conc_loads:
        load.start()

    barrier = pltpu.get_barrier_semaphore()
    for d in range(1, G):
        pl.semaphore_signal(barrier, inc=1, device_id=(lax.rem(g + d, G), j, i), device_id_type=MESH)
    for d in range(G):
        pl.semaphore_signal(barrier, inc=1, device_id=(d, j, i_east), device_id_type=MESH)
        pl.semaphore_signal(barrier, inc=1, device_id=(d, j, i_west), device_id_type=MESH)

    @pl.when(has_south)
    def _():
        for d in range(G):
            pl.semaphore_signal(barrier, inc=1, device_id=(d, j - 1, i), device_id_type=MESH)

    @pl.when(has_north)
    def _():
        for d in range(G):
            pl.semaphore_signal(barrier, inc=1, device_id=(d, j + 1, i), device_id_type=MESH)

    for load in loads:
        load.wait()
    lane = lanes((FOLDED, X))
    packed = jnp.zeros((FOLDED, X), jnp.float32)
    for p in range(PLANES):
        packed = jnp.where(lane // 2 == p, roll(planes[p, 8 : 8 + FOLDED, :], 2 * p + 1, 1), packed)
    edge_q[...] = packed

    around = lax.div(j + n_gy - 1, n_gy) + lax.div(2 * (n_gy - 1) - j, n_gy)
    pl.semaphore_wait(barrier, G - 1 + 2 * G + G * around)

    def remote(src, dst, n, device):
        return pltpu.make_async_remote_copy(
            src_ref=src,
            dst_ref=dst,
            send_sem=send_sem.at[n],
            recv_sem=recv_sem.at[n],
            device_id=device,
            device_id_type=MESH,
        )

    to_north = remote(planes.at[:, pl.ds(FOLDED, 8)], planes.at[:, pl.ds(0, 8)], 0, (g, j + 1, i))
    to_south = remote(
        planes.at[:, pl.ds(8, 8)], planes.at[:, pl.ds(8 + FOLDED, 8)], 1, (g, j - 1, i)
    )
    to_east = remote(edge_q, west_q, 2, (g, j, i_east))
    to_west = remote(edge_q, east_q, 3, (g, j, i_west))
    to_east.start()
    to_west.start()

    @pl.when(has_north)
    def _():
        to_north.start()

    @pl.when(has_south)
    def _():
        to_south.start()

    depth = jnp.where(land[...] > 0, bottom[...], 0).astype(jnp.float32)
    row_lo[pl.ds(T * Z, 8), :] = jnp.broadcast_to(depth[0:1], (8, X))
    row_hi[pl.ds(T * Z, 8), :] = jnp.broadcast_to(depth[Y - 1 : Y], (8, X))
    for n in range(CHUNKS):
        conc_loads[n].wait()

        def take_rows(t, carry):
            base = pl.multiple_of(t * (Z * Y), Z * Y)
            place = pl.multiple_of(t * Z, 8)
            row_lo[pl.ds(place, Z), :] = conc[pl.ds(base, Z, stride=Y), :]
            row_hi[pl.ds(place, Z), :] = conc[pl.ds(base + Y - 1, Z, stride=Y), :]
            return carry

        lax.fori_loop(n * (T // CHUNKS), (n + 1) * (T // CHUNKS), take_rows, 0)

    rows_north = remote(row_hi, south_rows, 4, (g, j + 1, i))
    rows_south = remote(row_lo, north_rows, 5, (g, j - 1, i))

    @pl.when(has_north)
    def _():
        rows_north.start()

    @pl.when(has_south)
    def _():
        rows_south.start()

    @pl.when(has_south)
    def _():
        to_north.wait_recv()

    @pl.when(has_north)
    def _():
        to_south.wait_recv()

    @pl.when(jnp.logical_not(has_south))
    def _():
        planes[:, pl.ds(0, 8), :] = jnp.zeros((PLANES, 8, X), jnp.float32)

    @pl.when(jnp.logical_not(has_north))
    def _():
        planes[:, pl.ds(8 + FOLDED, 8), :] = jnp.zeros((PLANES, 8, X), jnp.float32)

    to_east.wait_recv()
    to_west.wait_recv()
    fold = lax.rem(rows((FOLDED, X)), G)
    qw = west_q[...]
    qe = east_q[...]
    qw_turned = jnp.where(fold == 0, roll(qw, -(G - 1), 0), roll(qw, 1, 0))
    qe_turned = jnp.where(fold == G - 1, roll(qe, G - 1, 0), roll(qe, -1, 0))
    qw = jnp.where(i == 0, qw_turned, qw)
    qe = jnp.where(i == n_gx - 1, qe_turned, qe)
    west_q[...] = jnp.where(lane % 2 == 1, roll(qw, 1, 1), roll(qe, -1, 1))

    def eastern(x, edge):
        return jnp.where(lane == X - 1, edge, roll(x, -1, 1))

    def western(x, edge):
        return jnp.where(lane == 0, edge, roll(x, 1, 1))

    def sides(p):
        return roll(west_q[...], -(2 * p + 1), 1)

    def at(p, shift):
        return planes[p, 8 + shift : 8 + shift + FOLDED, :]

    height = at(2 * L, 0)
    push_east = GRAVITY * (eastern(height, sides(2 * L)) - height)
    push_north = GRAVITY * (at(2 * L, G) - height)
    spread = jnp.zeros((FOLDED, X), jnp.float32)
    pack = jnp.zeros((FOLDED, X), jnp.float32)
    for k in range(L):
        u = at(k, 0)
        v = at(L + k, 0)
        u_side = sides(k)
        v_side = sides(L + k)
        u_west = western(u, u_side)
        v_south = at(L + k, -G)
        lap_u = eastern(u, u_side) + u_west + at(k, G) + at(k, -G) - 4.0 * u
        lap_v = eastern(v, v_side) + western(v, v_side) + at(L + k, G) + v_south - 4.0 * v
        u_new = u + TIME_STEP * (CORIOLIS * v - push_east + VISCOSITY * lap_u)
        v_new = v + TIME_STEP * (-CORIOLIS * u - push_north + VISCOSITY * lap_v)
        spread = spread + (u - u_west + v - v_south)
        fresh[pl.ds(k * FOLDED, FOLDED), :] = u_new
        fresh[pl.ds((L + k) * FOLDED, FOLDED), :] = v_new
        pack = jnp.where(lane == k, roll(u_new, k + 1, 1), pack)
    col_pack[...] = pack
    for f in range(G):
        for p in range(2 * L):
            send_tile[f, pl.ds(p * Y, Y), :] = fresh[pl.ds(p * FOLDED + f, Y, stride=G), :]
        send_tile[f, pl.ds(TILE_ROWS, FOLDED), :] = spread
        send_u[f] = col_pack[pl.ds(f, Y, stride=G), :]
        send_v[f] = jnp.zeros((8, X), jnp.float32)
        send_v[f, pl.ds(0, L), :] = fresh[
            pl.ds(L * FOLDED + (Y - 1) * G + f, L, stride=FOLDED), :
        ]

    def tile_copy(d):
        other = lax.rem(g + d, G)
        return pltpu.make_async_remote_copy(
            src_ref=send_tile.at[other],
            dst_ref=tiles.at[g],
            send_sem=tile_send.at[other],
            recv_sem=tile_recv.at[g],
            device_id=(other, j, i),
            device_id_type=MESH,
        )

    def u_copy(f):
        crossed = jnp.where(i == n_gx - 1, 1, 0)
        return pltpu.make_async_remote_copy(
            src_ref=send_u.at[f],
            dst_ref=west_u.at[g],
            send_sem=u_send.at[f],
            recv_sem=u_recv.at[g],
            device_id=(lax.rem(f + crossed, G), j, i_east),
            device_id_type=MESH,
        )

    def v_copy(f):
        return pltpu.make_async_remote_copy(
            src_ref=send_v.at[f],
            dst_ref=south_v.at[g],
            send_sem=v_send.at[f],
            recv_sem=v_recv.at[g],
            device_id=(f, j + 1, i),
            device_id_type=MESH,
        )

    for d in (2, 1, 3):
        tile_copy(d).start()
    for f in range(G):
        u_copy(f).start()

    @pl.when(has_north)
    def _():
        for f in range(G):
            v_copy(f).start()

    own_tile = pltpu.make_async_copy(send_tile.at[g], tiles.at[g], store_sem.at[0])
    own_tile.start()

    small = lanes((8, X))

    def take_cols(z, carry):
        parts = [jnp.zeros((8, X), jnp.float32) for _ in range(4)]
        for t in range(T):
            for o in range(2):
                base = pl.multiple_of(t * (Z * Y) + z * Y + 8 * o, 8)
                n = (2 * t + o) % 4
                parts[n] = jnp.where(
                    small // 2 == 32 * o + t,
                    roll(conc[pl.ds(base, 8), :], 64 * o + 2 * t + 1, 1),
                    parts[n],
                )
        col_q[pl.ds(pl.multiple_of(z * 8, 8), 8), :] = (parts[0] + parts[1]) + (
            parts[2] + parts[3]
        )
        return carry

    lax.fori_loop(0, Z, take_cols, 0)
    col_q[pl.ds(Z * 8, 8), :] = jnp.where(
        small // 2 == 0,
        roll(depth[0:8], 1, 1),
        jnp.where(small // 2 == 32, roll(depth[8:16], 65, 1), 0.0),
    )
    up = jnp.where(i == n_gx - 1, 1, 0)
    down = jnp.where(i == 0, G - 1, 0)
    cols_east = remote(col_q, west_cols, 6, (lax.rem(g + up, G), j, i_east))
    cols_west = remote(col_q, east_cols, 7, (lax.rem(g + down, G), j, i_west))
    cols_east.start()
    cols_west.start()

    tall = (rows((8 * T, T)) // 8 == lanes((8 * T, T))).astype(jnp.bfloat16)
    wide = (rows((T, 8 * T)) == lanes((T, 8 * T)) // 8).astype(jnp.bfloat16)
    own = lax.rem(rows((8 * T, 8 * T)), 8) == lax.rem(lanes((8 * T, 8 * T)), 8)
    hi = coupling[...].astype(jnp.bfloat16)
    lo = (coupling[...] - hi.astype(jnp.float32)).astype(jnp.bfloat16)
    for part, place in ((hi, mix_hi), (lo, mix_lo)):
        half = jnp.dot(tall, part, preferred_element_type=jnp.float32).astype(jnp.bfloat16)
        whole = jnp.dot(half, wide, preferred_element_type=jnp.float32)
        place[...] = jnp.where(own, whole, 0.0).astype(jnp.bfloat16)
    stores = [
        pltpu.make_async_copy(mix_hi, mix_hi_out, store_sem.at[1]),
        pltpu.make_async_copy(mix_lo, mix_lo_out, store_sem.at[2]),
    ]
    for store in stores:
        store.start()

    for d in range(1, G):
        other = lax.rem(g + d, G)
        pltpu.make_async_remote_copy(
            src_ref=send_tile.at[other],
            dst_ref=tiles.at[other],
            send_sem=tile_send.at[other],
            recv_sem=tile_recv.at[other],
            device_id=(other, j, i),
            device_id_type=MESH,
        ).wait()
    for f in range(G):
        pltpu.make_async_remote_copy(
            src_ref=send_u.at[f],
            dst_ref=west_u.at[f],
            send_sem=u_send.at[f],
            recv_sem=u_recv.at[f],
            device_id=(f, j, i_east),
            device_id_type=MESH,
        ).wait()

    @pl.when(has_north)
    def _():
        to_north.wait_send()
        rows_north.wait_send()
        rows_south.wait_recv()
        for f in range(G):
            v_copy(f).wait_send()

    @pl.when(has_south)
    def _():
        to_south.wait_send()
        rows_south.wait_send()
        rows_north.wait_recv()
        for f in range(G):
            pltpu.make_async_remote_copy(
                src_ref=send_v.at[f],
                dst_ref=south_v.at[f],
                send_sem=v_send.at[f],
                recv_sem=v_recv.at[f],
                device_id=(f, j - 1, i),
                device_id_type=MESH,
            ).wait_recv()

    to_east.wait_send()
    to_west.wait_send()
    cols_east.wait()
    cols_west.wait()
    own_tile.wait()
    for store in stores:
        store.wait()


def exchange(n_gy, n_gx, u, v, eta, conc, land, bottom, coupling):
    f32 = jnp.float32
    dma = pltpu.SemaphoreType.DMA
    out_shape = (
        jax.ShapeDtypeStruct((G, TILE_ROWS + FOLDED, X), f32),
        jax.ShapeDtypeStruct((EDGE_ROWS, X), f32),
        jax.ShapeDtypeStruct((EDGE_ROWS, X), f32),
        jax.ShapeDtypeStruct((EDGE_COLS, X), f32),
        jax.ShapeDtypeStruct((EDGE_COLS, X), f32),
        jax.ShapeDtypeStruct((G, Y, X), f32),
        jax.ShapeDtypeStruct((G, 8, X), f32),
        jax.ShapeDtypeStruct((8 * T, 8 * T), jnp.bfloat16),
        jax.ShapeDtypeStruct((8 * T, 8 * T), jnp.bfloat16),
    )
    return pl.pallas_call(
        functools.partial(exchange_kernel, n_gy, n_gx),
        out_shape=out_shape,
        in_specs=[HBM] * 7,
        out_specs=(HBM,) * 9,
        scratch_shapes=[
            pltpu.VMEM((PLANES, FOLDED + 16, X), f32),
            pltpu.VMEM((T * Z * Y, X), f32),
            pltpu.VMEM((Y, X), jnp.int32),
            pltpu.VMEM((Y, X), jnp.int32),
            pltpu.VMEM((T, T), f32),
            pltpu.VMEM((FOLDED, X), f32),
            pltpu.VMEM((FOLDED, X), f32),
            pltpu.VMEM((FOLDED, X), f32),
            pltpu.VMEM((2 * L * FOLDED, X), f32),
            pltpu.VMEM((FOLDED, X), f32),
            pltpu.VMEM((G, TILE_ROWS + FOLDED, X), f32),
            pltpu.VMEM((G, Y, X), f32),
            pltpu.VMEM((G, 8, X), f32),
            pltpu.VMEM((EDGE_ROWS, X), f32),
            pltpu.VMEM((EDGE_ROWS, X), f32),
            pltpu.VMEM((EDGE_COLS, X), f32),
            pltpu.VMEM((8 * T, 8 * T), jnp.bfloat16),
            pltpu.VMEM((8 * T, 8 * T), jnp.bfloat16),
            dma((6,)),
            dma((CHUNKS,)),
            dma((8,)),
            dma((8,)),
            dma((G,)),
            dma((G,)),
            dma((G,)),
            dma((G,)),
            dma((G,)),
            dma((G,)),
            dma((3,)),
        ],
        compiler_params=pltpu.CompilerParams(
            collective_id=0, has_side_effects=True, vmem_limit_bytes=60 * 1024 * 1024
        ),
        name="exchange",
    )(u, v, eta, conc, land, bottom, coupling)


Z_PART = 4
T_PART = 5
COEF = 9


def column_kernel(
    n_gy,
    c_hbm,
    tiles_hbm,
    south_rows_hbm,
    north_rows_hbm,
    west_cols_hbm,
    east_cols_hbm,
    west_u_hbm,
    south_v_hbm,
    mix_hi_hbm,
    mix_lo_hbm,
    eta_hbm,
    land_hbm,
    bottom_hbm,
    out_hbm,
    surface_hbm,
    conc,
    solved,
    coef,
    tiles,
    south_rows,
    north_rows,
    west_cols,
    east_cols,
    west_u,
    south_v,
    mix_hi,
    mix_lo,
    eta,
    land,
    bottom,
    surface,
    adv_a,
    adv_b,
    hi_a,
    lo_a,
    hi_b,
    lo_b,
    load_sem,
    conc_sem,
    out_sem,
):
    j = lax.axis_index("gy")
    pairs = (
        (land_hbm, land),
        (bottom_hbm, bottom),
        (tiles_hbm, tiles),
        (west_u_hbm, west_u),
        (south_v_hbm, south_v),
        (west_cols_hbm, west_cols),
        (east_cols_hbm, east_cols),
        (south_rows_hbm, south_rows),
        (north_rows_hbm, north_rows),
        (eta_hbm, eta),
        (mix_hi_hbm, mix_hi),
        (mix_lo_hbm, mix_lo),
    )
    loads = [pltpu.make_async_copy(a, b, load_sem.at[n]) for n, (a, b) in enumerate(pairs)]
    for load in loads:
        load.start()
    conc_loads = [
        pltpu.make_async_copy(
            c_hbm.at[:, pl.ds(n * Z_PART, Z_PART)],
            conc.at[:, pl.ds(n * Z_PART, Z_PART), pl.ds(8, Y)],
            conc_sem.at[n],
        )
        for n in range(Z // Z_PART)
    ]
    for load in conc_loads:
        load.start()
    for load in loads:
        load.wait()

    flat = conc.reshape(T * Z * 32, X)
    south_ok = j > 0
    north_ok = j < n_gy - 1

    def put_rows(t, carry):
        place = pl.multiple_of(t * Z, 8)
        base = pl.multiple_of(t * (Z * 32), 8)
        flat[pl.ds(base + 7, Z, stride=32), :] = jnp.where(
            south_ok, south_rows[pl.ds(place, Z), :], 0.0
        )
        flat[pl.ds(base + 8 + Y, Z, stride=32), :] = jnp.where(
            north_ok, north_rows[pl.ds(place, Z), :], 0.0
        )
        return carry

    lax.fori_loop(0, T, put_rows, 0)

    lane = lanes((8, X))
    odd = lane % 2 == 1

    def put_cols(z, carry):
        place = pl.ds(pl.multiple_of(z * 8, 8), 8)
        west_cols[place, :] = jnp.where(
            odd, roll(west_cols[place, :], 1, 1), roll(east_cols[place, :], -1, 1)
        )
        return carry

    lax.fori_loop(0, Z + 1, put_cols, 0)

    total = tiles[0, pl.ds(TILE_ROWS, FOLDED), :]
    for m in range(1, G):
        total = total + tiles[m, pl.ds(TILE_ROWS, FOLDED), :]
    surface[...] = eta[...] - (BAROTROPIC / Z) * total
    surface_store = pltpu.make_async_copy(surface, surface_hbm, out_sem.at[T // T_PART])
    surface_store.start()

    wide = lanes((Y, X))
    tall = rows((Y, X))
    depth = jnp.where(land[...] > 0, bottom[...], 0).astype(jnp.float32)
    depth_side = west_cols[pl.ds(Z * 8, 8), :]
    depth_side = jnp.concatenate([roll(depth_side, -1, 1), roll(depth_side, -65, 1)], axis=0)
    depth_east = jnp.where(wide == X - 1, depth_side, roll(depth, -1, 1))
    depth_west = jnp.where(wide == 0, depth_side, roll(depth, 1, 1))
    above = jnp.where(north_ok, north_rows[pl.ds(T * Z, 8), :], 0.0)
    below = jnp.where(south_ok, south_rows[pl.ds(T * Z, 8), :], 0.0)
    depth_north = jnp.where(
        tall == Y - 1, jnp.concatenate([above, above], axis=0), roll(depth, -1, 0)
    )
    depth_south = jnp.where(tall == 0, jnp.concatenate([below, below], axis=0), roll(depth, 1, 0))
    reach_east = jnp.minimum(depth, depth_east)
    reach_west = jnp.minimum(depth, depth_west)
    reach_north = jnp.minimum(depth, depth_north)
    reach_south = jnp.minimum(depth, depth_south)

    def flows(z):
        m, k = z // L, z % L
        return tiles[m, pl.ds(k * Y, Y), :], tiles[m, pl.ds((L + k) * Y, Y), :]

    g_above = jnp.zeros((Y, X), jnp.float32)
    r_above = jnp.zeros((Y, X), jnp.float32)
    u, v = flows(0)
    for z in range(Z):
        m, k = z // L, z % L
        u_west = jnp.where(wide == 0, roll(west_u[m], -k, 1), roll(u, 1, 1))
        row = jnp.where(south_ok, south_v[m, k : k + 1, :], 0.0)
        v_south = jnp.where(tall == 0, jnp.broadcast_to(row, (Y, X)), roll(v, 1, 0))
        ke = jnp.where(reach_east > z, ADVECTION, 0.0)
        kw = jnp.where(reach_west > z, ADVECTION, 0.0)
        kn = jnp.where(reach_north > z, ADVECTION, 0.0)
        ks = jnp.where(reach_south > z, ADVECTION, 0.0)
        coef[z, 0] = (
            1.0
            - ke * jnp.maximum(u, 0.0)
            + kw * jnp.minimum(u_west, 0.0)
            - kn * jnp.maximum(v, 0.0)
            + ks * jnp.minimum(v_south, 0.0)
        )
        coef[z, 1] = -ke * jnp.minimum(u, 0.0)
        coef[z, 2] = kw * jnp.maximum(u_west, 0.0)
        coef[z, 3] = -kn * jnp.minimum(v, 0.0)
        coef[z, 4] = ks * jnp.maximum(v_south, 0.0)
        if z < Z - 1:
            u_next, v_next = flows(z + 1)
            shear = (u - u_next) ** 2 + (v - v_next) ** 2
            rate = KAPPA_BASE + KAPPA_SHEAR * shear / (shear + SHEAR_SCALE)
            g = jnp.where(depth > z + 1, MIXING * rate, 0.0)
            u, v = u_next, v_next
        else:
            g = jnp.zeros((Y, X), jnp.float32)
        inverse = 1.0 / (1.0 + g_above + g - g_above * r_above)
        coef[z, 5] = inverse
        coef[z, 6] = jnp.where(depth > z, ECOLOGY * inverse, 0.0)
        coef[z, 7] = g_above * inverse
        r_above = g * inverse
        coef[z, 8] = r_above
        g_above = g

    def zero_top(t, carry):
        solved[t, 0] = jnp.zeros((Y, X), jnp.float32)
        return carry

    lax.fori_loop(0, T, zero_top, 0)

    def advance(z, adv, hi_ref, lo_ref):
        side = west_cols[pl.ds(pl.multiple_of(z * 8, 8), 8), :]
        for o in range(2):
            ks = [coef[z, n, 8 * o : 8 * o + 8, :] for n in range(5)]
            for pair in range(T // 2):
                both = []
                for t in (2 * pair, 2 * pair + 1):
                    c = conc[t, z, 8 + 8 * o : 16 + 8 * o, :]
                    edge = roll(side, -(64 * o + 2 * t + 1), 1)
                    east = jnp.where(lane == X - 1, edge, roll(c, -1, 1))
                    west = jnp.where(lane == 0, edge, roll(c, 1, 1))
                    north = conc[t, z, 9 + 8 * o : 17 + 8 * o, :]
                    south = conc[t, z, 7 + 8 * o : 15 + 8 * o, :]
                    a = (ks[0] * c + ks[1] * east) + (
                        ks[2] * west + (ks[3] * north + ks[4] * south)
                    )
                    adv[t, 8 * o : 8 * o + 8, :] = a
                    both.append(jnp.tanh(a))
                y = jnp.concatenate(both, axis=0)
                hi = y.astype(jnp.bfloat16)
                lo = (y - hi.astype(jnp.float32)).astype(jnp.bfloat16)
                hi_ref[16 * pair : 16 * pair + 16, o * X : o * X + X] = hi
                lo_ref[16 * pair : 16 * pair + 16, o * X : o * X + X] = lo

    def mix(hi_ref, lo_ref):
        return (
            jnp.dot(mix_hi[...], hi_ref[...], preferred_element_type=jnp.float32)
            + jnp.dot(mix_lo[...], hi_ref[...], preferred_element_type=jnp.float32)
            + jnp.dot(mix_hi[...], lo_ref[...], preferred_element_type=jnp.float32)
        )

    def finish(z, adv, source):
        for o in range(2):
            ks = [coef[z, n, 8 * o : 8 * o + 8, :] for n in range(5, 8)]
            for t in range(T):
                s = source[8 * t : 8 * t + 8, o * X : o * X + X]
                solved[t, z + 1, 8 * o : 8 * o + 8, :] = (
                    ks[0] * adv[t, 8 * o : 8 * o + 8, :]
                    + ks[1] * s
                    + ks[2] * solved[t, z, 8 * o : 8 * o + 8, :]
                )

    def two(i, carry):
        z = 2 * i

        source = mix(hi_a, lo_a)
        advance(z + 1, adv_b, hi_b, lo_b)
        finish(z, adv_a, source)
        source = mix(hi_b, lo_b)
        advance(z + 2, adv_a, hi_a, lo_a)
        finish(z + 1, adv_b, source)
        return carry

    for load in conc_loads:
        load.wait()
    advance(0, adv_a, hi_a, lo_a)
    lax.fori_loop(0, Z // 2 - 1, two, 0)
    source = mix(hi_a, lo_a)
    advance(Z - 1, adv_b, hi_b, lo_b)
    finish(Z - 2, adv_a, source)
    finish(Z - 1, adv_b, mix(hi_b, lo_b))

    def store(n):
        return pltpu.make_async_copy(
            solved.at[pl.ds(n * T_PART, T_PART), pl.ds(1, Z)],
            out_hbm.at[pl.ds(n * T_PART, T_PART)],
            out_sem.at[n],
        )

    def back(n, carry):
        base = n * T_PART
        x = [solved[base + t, Z] for t in range(T_PART)]
        for z in range(Z - 2, -1, -1):
            r = coef[z, 8]
            for t in range(T_PART):
                x[t] = solved[base + t, z + 1] + r * x[t]
                solved[base + t, z + 1] = x[t]
        store(n).start()
        return carry

    lax.fori_loop(0, T // T_PART, back, 0)
    for n in range(T // T_PART):
        store(n).wait()
    surface_store.wait()


def columns(n_gy, conc, parts, eta, land, bottom):
    f32 = jnp.float32
    dma = pltpu.SemaphoreType.DMA
    mix_type = pltpu.VMEM((8 * T, 2 * X), jnp.bfloat16)
    return pl.pallas_call(
        functools.partial(column_kernel, n_gy),
        out_shape=(
            jax.ShapeDtypeStruct((T, Z, Y, X), f32),
            jax.ShapeDtypeStruct((FOLDED, X), f32),
        ),
        in_specs=[HBM] * 13,
        out_specs=(HBM, HBM),
        scratch_shapes=[
            pltpu.VMEM((T, Z, 32, X), f32),
            pltpu.VMEM((T, Z + 1, Y, X), f32),
            pltpu.VMEM((Z, COEF, Y, X), f32),
            pltpu.VMEM((G, TILE_ROWS + FOLDED, X), f32),
            pltpu.VMEM((EDGE_ROWS, X), f32),
            pltpu.VMEM((EDGE_ROWS, X), f32),
            pltpu.VMEM((EDGE_COLS, X), f32),
            pltpu.VMEM((EDGE_COLS, X), f32),
            pltpu.VMEM((G, Y, X), f32),
            pltpu.VMEM((G, 8, X), f32),
            pltpu.VMEM((8 * T, 8 * T), jnp.bfloat16),
            pltpu.VMEM((8 * T, 8 * T), jnp.bfloat16),
            pltpu.VMEM((FOLDED, X), f32),
            pltpu.VMEM((Y, X), jnp.int32),
            pltpu.VMEM((Y, X), jnp.int32),
            pltpu.VMEM((FOLDED, X), f32),
            pltpu.VMEM((T, Y, X), f32),
            pltpu.VMEM((T, Y, X), f32),
            mix_type,
            mix_type,
            mix_type,
            mix_type,
            dma((12,)),
            dma((Z // Z_PART,)),
            dma((T // T_PART + 1,)),
        ],
        compiler_params=pltpu.CompilerParams(vmem_limit_bytes=60 * 1024 * 1024),
        name="columns",
    )(conc, *parts, eta, land, bottom)


def shards(east_velocity, north_velocity, sea_surface, tracers, land_sea, bottom_level, coupling):
    n_gy = lax.axis_size("gy")
    n_gx = lax.axis_size("gx")
    eta = sea_surface.reshape(FOLDED, X)
    parts = exchange(
        n_gy,
        n_gx,
        east_velocity.reshape(L, FOLDED, X),
        north_velocity.reshape(L, FOLDED, X),
        eta,
        tracers.reshape(T * Z * Y, X),
        land_sea,
        bottom_level,
        coupling,
    )
    tracers_next, surface_next = columns(n_gy, tracers, parts, eta, land_sea, bottom_level)
    return tracers_next, surface_next.reshape(Y, G, X)


def solution(mesh):
    placed = (
        P("group", "gy", None, "gx"),
        P("group", "gy", None, "gx"),
        P("gy", None, "gx"),
        P(None, None, "gy", ("group", "gx")),
        P("gy", ("group", "gx")),
        P("gy", ("group", "gx")),
        P(),
    )
    return jax.shard_map(
        shards,
        mesh=mesh,
        in_specs=placed,
        out_specs=(P(None, None, "gy", ("group", "gx")), P("gy", None, "gx")),
        check_vma=False,
    )
```

```python
import functools

import jax
import jax.numpy as jnp
from jax import lax
from jax.experimental import pallas as pl
from jax.experimental.pallas import tpu as pltpu
from jax.sharding import PartitionSpec as P

CORIOLIS = 0.5
GRAVITY = 0.3
VISCOSITY = 0.1
TIME_STEP = 0.2
BAROTROPIC = 0.5
ADVECTION = 0.15
MIXING = 0.5
KAPPA_BASE = 0.1
KAPPA_SHEAR = 2.0
SHEAR_SCALE = 1.0
ECOLOGY = 0.2

MESH = pl.DeviceIdType.MESH
HBM = pl.BlockSpec(memory_space=pltpu.HBM)

T = 30
Z = 24
G = 4
L = Z // G
Y = 16
X = 128
PLANES = 2 * L + 1
FOLDED = Y * G
TILE_ROWS = 2 * L * Y
EDGE_ROWS = T * Z + 8
EDGE_COLS = Z // 2 * 8 + 8


def roll(x, by, axis):
    by = by % x.shape[axis]
    return x if by == 0 else pltpu.roll(x, by, axis)


def lanes(shape):
    return lax.broadcasted_iota(jnp.int32, shape, len(shape) - 1)


def rows(shape):
    return lax.broadcasted_iota(jnp.int32, shape, 0)


def exchange_kernel(
    n_gy,
    n_gx,
    u_hbm,
    v_hbm,
    eta_hbm,
    c_hbm,
    land_hbm,
    bottom_hbm,
    coupling_hbm,
    flow_u_out,
    flow_v_out,
    west_u_out,
    south_v_out,
    south_rows,
    north_rows,
    west_cols,
    east_cols,
    mix_hi_out,
    mix_lo_out,
    surface_out,
    planes,
    conc,
    land,
    bottom,
    coupling,
    edge_q,
    west_q,
    east_q,
    send_tile,
    send_up,
    send_down,
    send_col,
    tiles,
    from_south,
    from_north,
    from_west,
    from_east,
    from_sw,
    from_nw,
    from_se,
    spread_sum,
    spreads,
    push,
    flow_u,
    flow_v,
    west_u,
    south_v,
    row_lo,
    row_hi,
    col_east,
    col_west,
    mix_hi,
    mix_lo,
    surface,
    load_sem,
    conc_sem,
    send_sem,
    recv_sem,
    group_send,
    group_recv,
    store_sem,
):
    g = lax.axis_index("group")
    j = lax.axis_index("gy")
    i = lax.axis_index("gx")
    i_east = lax.rem(i + 1, n_gx)
    i_west = lax.rem(i + n_gx - 1, n_gx)
    has_south = j > 0
    has_north = j < n_gy - 1
    up = lax.div(i + 1, n_gx)
    down = (1 - lax.div(i + n_gx - 1, n_gx)) * (G - 1)

    loads = [
        pltpu.make_async_copy(u_hbm, planes.at[pl.ds(0, L), pl.ds(8, FOLDED)], load_sem.at[0]),
        pltpu.make_async_copy(v_hbm, planes.at[pl.ds(L, L), pl.ds(8, FOLDED)], load_sem.at[1]),
        pltpu.make_async_copy(eta_hbm, planes.at[2 * L, pl.ds(8, FOLDED)], load_sem.at[2]),
        pltpu.make_async_copy(land_hbm, land, load_sem.at[3]),
        pltpu.make_async_copy(bottom_hbm, bottom, load_sem.at[4]),
        pltpu.make_async_copy(coupling_hbm, coupling, load_sem.at[5]),
    ]
    for load in loads:
        load.start()
    conc_load = pltpu.make_async_copy(c_hbm, conc, conc_sem.at[0])
    conc_load.start()

    barrier = pltpu.get_barrier_semaphore()

    def greet(*device):
        pl.semaphore_signal(barrier, inc=1, device_id=device, device_id_type=MESH)

    for d in range(G):
        greet(d, j, i_east)
        greet(d, j, i_west)

    @pl.when(has_south)
    def _():
        for d in range(G):
            greet(d, j - 1, i_west)
            greet(d, j - 1, i_east)
            greet(d, j - 1, i)

    @pl.when(has_north)
    def _():
        for d in range(G):
            greet(d, j + 1, i_west)
            greet(d, j + 1, i)

    for d in range(1, G):
        greet(lax.rem(g + d, G), j, i)

    for load in loads:
        load.wait()
    lane = lanes((FOLDED, X))
    packed = jnp.zeros((FOLDED, X), jnp.float32)
    for p in range(PLANES):
        packed = jnp.where(lane // 4 == p, roll(planes[p, 8 : 8 + FOLDED, :], 4 * p + 2, 1), packed)
    edge_q[...] = packed
    flat = planes.reshape(PLANES * (FOLDED + 16), X)
    step = FOLDED + 16
    v_at = L * step
    top = 8 + (Y - 1) * G
    for f in range(G):
        send_col[f] = edge_q[pl.ds(f, Y, stride=G), :]
        send_up[f] = jnp.zeros((24, X), jnp.float32)
        send_up[f, pl.ds(0, L), :] = flat[pl.ds(top + f, L, stride=step), :]
        send_up[f, pl.ds(L, L), :] = flat[pl.ds(v_at + top + f, L, stride=step), :]
        send_up[f, pl.ds(2 * L, L), :] = flat[pl.ds(v_at + top - G + f, L, stride=step), :]
        send_down[f] = jnp.zeros((16, X), jnp.float32)
        send_down[f, pl.ds(0, L), :] = flat[pl.ds(8 + f, L, stride=step), :]
        send_down[f, pl.ds(L, L), :] = flat[pl.ds(v_at + 8 + f, L, stride=step), :]
        for p in range(2 * L):
            send_tile[f, pl.ds(p * Y, Y), :] = flat[pl.ds(p * step + 8 + f, Y, stride=G), :]

    south_count = lax.div(j + n_gy - 1, n_gy)
    north_count = lax.div(2 * (n_gy - 1) - j, n_gy)
    pl.semaphore_wait(barrier, G - 1 + 2 * G + 2 * G * south_count + 3 * G * north_count)

    def remote(src, dst, n, device):
        return pltpu.make_async_remote_copy(
            src_ref=src,
            dst_ref=dst,
            send_sem=send_sem.at[n],
            recv_sem=recv_sem.at[n],
            device_id=device,
            device_id_type=MESH,
        )

    def spread_out(kind, src, dst, f, m, device):
        return pltpu.make_async_remote_copy(
            src_ref=src,
            dst_ref=dst.at[m],
            send_sem=group_send.at[kind, f],
            recv_sem=group_recv.at[kind, m],
            device_id=device,
            device_id_type=MESH,
        )

    def corner_ne(f, m):
        device = (lax.rem(f + up, G), j + 1, i_east)
        return spread_out(0, send_col.at[f, pl.ds(8, 8)], from_sw, f, m, device)

    def corner_se(f, m):
        device = (lax.rem(f + up, G), j - 1, i_east)
        return spread_out(1, send_col.at[f, pl.ds(0, 8)], from_nw, f, m, device)

    def corner_nw(f, m):
        device = (lax.rem(f + down, G), j + 1, i_west)
        return spread_out(2, send_col.at[f, pl.ds(8, 8)], from_se, f, m, device)

    def col_to_east(f, m):
        return spread_out(
            3, send_col.at[f], from_west, f, m, (lax.rem(f + up, G), j, i_east)
        )

    def col_to_west(f, m):
        return spread_out(
            4, send_col.at[f], from_east, f, m, (lax.rem(f + down, G), j, i_west)
        )

    def row_to_north(f, m):
        return spread_out(5, send_up.at[f], from_south, f, m, (f, j + 1, i))

    def row_to_south(f, m):
        return spread_out(6, send_down.at[f], from_north, f, m, (f, j - 1, i))

    def tile_to(f, m):
        return spread_out(7, send_tile.at[f], tiles, f, m, (f, j, i))

    def part_to(f, m):
        return spread_out(8, spread_sum, spreads, f, m, (f, j, i))

    to_north = remote(
        planes.at[pl.ds(L, L + 1), pl.ds(FOLDED, 8)],
        planes.at[pl.ds(L, L + 1), pl.ds(0, 8)],
        0,
        (g, j + 1, i),
    )
    to_south = remote(
        planes.at[2 * L, pl.ds(8, 8)], planes.at[2 * L, pl.ds(8 + FOLDED, 8)], 1, (g, j - 1, i)
    )
    to_east = remote(edge_q, west_q, 2, (g, j, i_east))
    to_west = remote(edge_q, east_q, 3, (g, j, i_west))
    rows_north = remote(row_hi, south_rows, 4, (g, j + 1, i))
    rows_south = remote(row_lo, north_rows, 5, (g, j - 1, i))
    cols_east = remote(col_east, west_cols, 6, (lax.rem(g + up, G), j, i_east))
    cols_west = remote(col_west, east_cols, 7, (lax.rem(g + down, G), j, i_west))

    @pl.when(has_north)
    def _():
        for f in range(G):
            corner_ne(f, g).start()
            corner_nw(f, g).start()

    @pl.when(has_south)
    def _():
        for f in range(G):
            corner_se(f, g).start()

    for f in range(G):
        col_to_east(f, g).start()
        col_to_west(f, g).start()
    to_east.start()
    to_west.start()
    for d in (2, 1, 3):
        tile_to(lax.rem(g + d, G), g).start()

    @pl.when(has_north)
    def _():
        to_north.start()
        for f in range(G):
            row_to_north(f, g).start()

    @pl.when(has_south)
    def _():
        to_south.start()
        for f in range(G):
            row_to_south(f, g).start()

    tiles[g] = send_tile[g]

    depth = jnp.where(land[...] > 0, bottom[...], 0).astype(jnp.float32)
    conc_load.wait()
    small = lanes((8, X))

    def take_cols(pair, carry):
        to_e = [jnp.zeros((8, X), jnp.float32) for _ in range(4)]
        to_w = [jnp.zeros((8, X), jnp.float32) for _ in range(4)]
        for half in range(2):
            for t in range(T):
                for o in range(2):
                    base = pl.multiple_of((t * Z + 2 * pair + half) * Y + 8 * o, 8)
                    spot = 64 * o + 2 * t + half
                    turned = roll(conc[pl.ds(base, 8), :], spot + 1, 1)
                    n = (2 * t + o) % 4
                    to_e[n] = jnp.where(small == spot, turned, to_e[n])
                    to_w[n] = jnp.where(small == spot + 1, turned, to_w[n])
        place = pl.ds(pl.multiple_of(pair * 8, 8), 8)
        col_east[place, :] = (to_e[0] + to_e[1]) + (to_e[2] + to_e[3])
        col_west[place, :] = roll((to_w[0] + to_w[1]) + (to_w[2] + to_w[3]), -1, 1)
        return carry

    lax.fori_loop(0, Z // 2, take_cols, 0)
    last = pl.ds(Z // 2 * 8, 8)
    col_east[last, :] = jnp.where(small < 64, roll(depth[0:8], 1, 1), roll(depth[8:16], 65, 1))
    col_west[last, :] = jnp.where(small < 64, depth[0:8], roll(depth[8:16], 64, 1))
    cols_east.start()
    cols_west.start()

    row_lo[pl.ds(T * Z, 8), :] = jnp.broadcast_to(depth[0:1], (8, X))
    row_hi[pl.ds(T * Z, 8), :] = jnp.broadcast_to(depth[Y - 1 : Y], (8, X))

    def take_rows(t, carry):
        base = pl.multiple_of(t * (Z * Y), Z * Y)
        place = pl.multiple_of(t * Z, 8)
        row_lo[pl.ds(place, Z), :] = conc[pl.ds(base, Z, stride=Y), :]
        row_hi[pl.ds(place, Z), :] = conc[pl.ds(base + Y - 1, Z, stride=Y), :]
        return carry

    lax.fori_loop(0, T, take_rows, 0)

    @pl.when(has_north)
    def _():
        rows_north.start()

    @pl.when(has_south)
    def _():
        rows_south.start()

    tall = (rows((8 * T, T)) // 8 == lanes((8 * T, T))).astype(jnp.bfloat16)
    wide = (rows((T, 8 * T)) == lanes((T, 8 * T)) // 8).astype(jnp.bfloat16)
    own = lax.rem(rows((8 * T, 8 * T)), 8) == lax.rem(lanes((8 * T, 8 * T)), 8)
    hi = coupling[...].astype(jnp.bfloat16)
    lo = (coupling[...] - hi.astype(jnp.float32)).astype(jnp.bfloat16)
    for part, place in ((hi, mix_hi), (lo, mix_lo)):
        half = jnp.dot(tall, part, preferred_element_type=jnp.float32).astype(jnp.bfloat16)
        whole = jnp.dot(half, wide, preferred_element_type=jnp.float32)
        place[...] = jnp.where(own, whole, 0.0).astype(jnp.bfloat16)
    stores = [
        pltpu.make_async_copy(mix_hi, mix_hi_out, store_sem.at[0]),
        pltpu.make_async_copy(mix_lo, mix_lo_out, store_sem.at[1]),
    ]
    for store in stores:
        store.start()

    @pl.when(has_south)
    def _():
        to_north.wait_recv()

    @pl.when(has_north)
    def _():
        to_south.wait_recv()

    @pl.when(jnp.logical_not(has_south))
    def _():
        planes[pl.ds(L, L + 1), pl.ds(0, 8), :] = jnp.zeros((L + 1, 8, X), jnp.float32)

    @pl.when(jnp.logical_not(has_north))
    def _():
        planes[2 * L, pl.ds(8 + FOLDED, 8), :] = jnp.zeros((8, X), jnp.float32)

    to_east.wait_recv()
    to_west.wait_recv()
    fold = lax.rem(rows((FOLDED, X)), G)
    qw = west_q[...]
    qe = east_q[...]
    qw_turned = jnp.where(fold == 0, roll(qw, -(G - 1), 0), roll(qw, 1, 0))
    qe_turned = jnp.where(fold == G - 1, roll(qe, G - 1, 0), roll(qe, -1, 0))
    qw = jnp.where(i == 0, qw_turned, qw)
    qe = jnp.where(i == n_gx - 1, qe_turned, qe)
    spread = jnp.zeros((FOLDED, X), jnp.float32)
    for k in range(L):
        u = planes[k, 8 : 8 + FOLDED, :]
        v = planes[L + k, 8 : 8 + FOLDED, :]
        u_west = jnp.where(lane == 0, roll(qw, -(4 * k + 1), 1), roll(u, 1, 1))
        spread = spread + (u - u_west + v - planes[L + k, 8 - G : 8 - G + FOLDED, :])
    spread_sum[...] = spread
    for d in (2, 1, 3):
        part_to(lax.rem(g + d, G), g).start()
    spreads[g] = spread

    e = 4 * (2 * L)
    height = planes[2 * L, 8 : 8 + FOLDED, :]
    height_east = jnp.where(lane == X - 1, roll(qe, X - 1 - (e + 2), 1), roll(height, -1, 1))
    push[0:FOLDED, :] = GRAVITY * (height_east - height)
    push[FOLDED : 2 * FOLDED, :] = GRAVITY * (height - roll(qw, -(e + 1), 1))
    push[2 * FOLDED : 3 * FOLDED, :] = GRAVITY * (
        planes[2 * L, 8 + G : 8 + G + FOLDED, :] - height
    )
    push[3 * FOLDED : 3 * FOLDED + 8, :] = GRAVITY * (
        planes[2 * L, 8:16, :] - planes[2 * L, 8 - G : 16 - G, :]
    )
    push_east = push[pl.ds(g, Y, stride=G), :]
    push_west = push[pl.ds(FOLDED + g, Y, stride=G), :]
    push_west = jnp.broadcast_to(push_west[:, 0:1], (Y, X))
    push_north = push[pl.ds(2 * FOLDED + g, Y, stride=G), :]
    push_south = jnp.broadcast_to(push[pl.ds(3 * FOLDED + g, 1), :], (8, X))

    for d in range(1, G):
        tile_to(lax.rem(g + d, G), lax.rem(g + d, G)).wait_recv()
    for m in range(G):
        col_to_east(m, m).wait_recv()
        col_to_west(m, m).wait_recv()

    @pl.when(has_south)
    def _():
        for m in range(G):
            corner_ne(m, m).wait_recv()
            corner_nw(m, m).wait_recv()
            row_to_north(m, m).wait_recv()

    @pl.when(has_north)
    def _():
        for m in range(G):
            corner_se(m, m).wait_recv()
            row_to_south(m, m).wait_recv()

    line = lanes((Y, X))
    deep = rows((Y, X))

    def over(row, shape=(Y, X)):
        return jnp.broadcast_to(row, shape)

    for m in range(G):
        south = jnp.where(has_south, from_south[m], 0.0)
        north = jnp.where(has_north, from_north[m], 0.0)
        sw = jnp.where(has_south, from_sw[m], 0.0)[7:8]
        se = jnp.where(has_south, from_se[m], 0.0)[7:8]
        nw = jnp.where(has_north, from_nw[m], 0.0)[0:1]
        west = from_west[m]
        side = jnp.where(line % 4 == 1, west, roll(from_east[m], -2, 1))
        first = jnp.zeros((Y, X), jnp.float32)
        below = jnp.zeros((8, X), jnp.float32)
        sw8 = over(sw, (8, X))
        se8 = over(se, (8, X))
        for k in range(L):
            u = tiles[m, pl.ds(k * Y, Y), :]
            v = tiles[m, pl.ds((L + k) * Y, Y), :]

            def laplacian(x, p):
                edge = roll(side, -(4 * p + 1), 1)
                return (
                    jnp.where(line == X - 1, edge, roll(x, -1, 1))
                    + jnp.where(line == 0, edge, roll(x, 1, 1))
                    + jnp.where(deep == Y - 1, over(north[p : p + 1]), roll(x, -1, 0))
                    + jnp.where(deep == 0, over(south[p : p + 1]), roll(x, 1, 0))
                    - 4.0 * x
                )

            flow_u[m * L + k] = u + TIME_STEP * (
                CORIOLIS * v - push_east + VISCOSITY * laplacian(u, k)
            )
            flow_v[m * L + k] = v + TIME_STEP * (
                -CORIOLIS * u - push_north + VISCOSITY * laplacian(v, L + k)
            )
            spot = 4 * k + 1
            first = jnp.where(line == spot, roll(u, spot, 1), first)
            p = L + k
            a = over(south[p : p + 1], (8, X))
            lap = (
                jnp.where(small == X - 1, roll(se8, X - 1 - (4 * p + 2), 1), roll(a, -1, 1))
                + jnp.where(small == 0, roll(sw8, -(4 * p + 1), 1), roll(a, 1, 1))
                + over(v[0:1], (8, X))
                + over(south[2 * L + k : 2 * L + k + 1], (8, X))
                - 4.0 * a
            )
            a = a + TIME_STEP * (
                -CORIOLIS * over(south[k : k + 1], (8, X)) - push_south + VISCOSITY * lap
            )
            below = jnp.where(rows((8, X)) == k, a, below)
        south_v[m] = below
        west_north = jnp.where(deep == Y - 1, over(nw), roll(west, -1, 0))
        west_south = jnp.where(deep == 0, over(sw), roll(west, 1, 0))
        lap = first + roll(west, 1, 1) + west_north + west_south - 4.0 * west
        west_u[m] = west + TIME_STEP * (
            CORIOLIS * roll(west, -4 * L, 1) - push_west + VISCOSITY * lap
        )
    flows = [
        pltpu.make_async_copy(flow_u, flow_u_out, store_sem.at[2]),
        pltpu.make_async_copy(flow_v, flow_v_out, store_sem.at[3]),
        pltpu.make_async_copy(west_u, west_u_out, store_sem.at[4]),
        pltpu.make_async_copy(south_v, south_v_out, store_sem.at[5]),
    ]
    for store in flows:
        store.start()

    for d in range(1, G):
        part_to(lax.rem(g + d, G), lax.rem(g + d, G)).wait_recv()
    surface[...] = planes[2 * L, 8 : 8 + FOLDED, :] - (BAROTROPIC / Z) * (
        (spreads[0] + spreads[1]) + (spreads[2] + spreads[3])
    )
    surface_store = pltpu.make_async_copy(surface, surface_out, store_sem.at[6])
    surface_store.start()

    for d in range(1, G):
        tile_to(lax.rem(g + d, G), g).wait_send()
        part_to(lax.rem(g + d, G), g).wait_send()
    for f in range(G):
        col_to_east(f, g).wait_send()
        col_to_west(f, g).wait_send()

    @pl.when(has_north)
    def _():
        to_north.wait_send()
        rows_north.wait_send()
        rows_south.wait_recv()
        for f in range(G):
            row_to_north(f, g).wait_send()
            corner_ne(f, g).wait_send()
            corner_nw(f, g).wait_send()

    @pl.when(has_south)
    def _():
        to_south.wait_send()
        rows_south.wait_send()
        rows_north.wait_recv()
        for f in range(G):
            row_to_south(f, g).wait_send()
            corner_se(f, g).wait_send()

    to_east.wait_send()
    to_west.wait_send()
    cols_east.wait()
    cols_west.wait()
    for store in stores + flows:
        store.wait()
    surface_store.wait()


def exchange(n_gy, n_gx, u, v, eta, conc, land, bottom, coupling):
    f32 = jnp.float32
    dma = pltpu.SemaphoreType.DMA
    mix = ((8 * T, 8 * T), jnp.bfloat16)
    out_shape = tuple(
        jax.ShapeDtypeStruct(*shape)
        for shape in (
            ((Z, Y, X), f32),
            ((Z, Y, X), f32),
            ((G, Y, X), f32),
            ((G, 8, X), f32),
            ((EDGE_ROWS, X), f32),
            ((EDGE_ROWS, X), f32),
            ((EDGE_COLS, X), f32),
            ((EDGE_COLS, X), f32),
            mix,
            mix,
            ((FOLDED, X), f32),
        )
    )
    return pl.pallas_call(
        functools.partial(exchange_kernel, n_gy, n_gx),
        out_shape=out_shape,
        in_specs=[HBM] * 7,
        out_specs=(HBM,) * len(out_shape),
        scratch_shapes=[
            pltpu.VMEM((PLANES, FOLDED + 16, X), f32),
            pltpu.VMEM((T * Z * Y, X), f32),
            pltpu.VMEM((Y, X), jnp.int32),
            pltpu.VMEM((Y, X), jnp.int32),
            pltpu.VMEM((T, T), f32),
            pltpu.VMEM((FOLDED, X), f32),
            pltpu.VMEM((FOLDED, X), f32),
            pltpu.VMEM((FOLDED, X), f32),
            pltpu.VMEM((G, TILE_ROWS, X), f32),
            pltpu.VMEM((G, 24, X), f32),
            pltpu.VMEM((G, 16, X), f32),
            pltpu.VMEM((G, Y, X), f32),
            pltpu.VMEM((G, TILE_ROWS, X), f32),
            pltpu.VMEM((G, 24, X), f32),
            pltpu.VMEM((G, 16, X), f32),
            pltpu.VMEM((G, Y, X), f32),
            pltpu.VMEM((G, Y, X), f32),
            pltpu.VMEM((G, 8, X), f32),
            pltpu.VMEM((G, 8, X), f32),
            pltpu.VMEM((G, 8, X), f32),
            pltpu.VMEM((FOLDED, X), f32),
            pltpu.VMEM((G, FOLDED, X), f32),
            pltpu.VMEM((3 * FOLDED + 8, X), f32),
            pltpu.VMEM((Z, Y, X), f32),
            pltpu.VMEM((Z, Y, X), f32),
            pltpu.VMEM((G, Y, X), f32),
            pltpu.VMEM((G, 8, X), f32),
            pltpu.VMEM((EDGE_ROWS, X), f32),
            pltpu.VMEM((EDGE_ROWS, X), f32),
            pltpu.VMEM((EDGE_COLS, X), f32),
            pltpu.VMEM((EDGE_COLS, X), f32),
            pltpu.VMEM(*mix),
            pltpu.VMEM(*mix),
            pltpu.VMEM((FOLDED, X), f32),
            dma((6,)),
            dma((1,)),
            dma((8,)),
            dma((8,)),
            dma((9, G)),
            dma((9, G)),
            dma((7,)),
        ],
        compiler_params=pltpu.CompilerParams(
            collective_id=0, has_side_effects=True, vmem_limit_bytes=60 * 1024 * 1024
        ),
        name="exchange",
    )(u, v, eta, conc, land, bottom, coupling)


Z_PART = 4
T_PART = 5
COEF = 9


def column_kernel(
    n_gy,
    c_hbm,
    flow_u_hbm,
    flow_v_hbm,
    west_u_hbm,
    south_v_hbm,
    south_rows_hbm,
    north_rows_hbm,
    west_cols_hbm,
    east_cols_hbm,
    mix_hi_hbm,
    mix_lo_hbm,
    surface_in,
    land_hbm,
    bottom_hbm,
    out_hbm,
    surface_hbm,
    conc,
    solved,
    coef,
    flow_u,
    flow_v,
    south_rows,
    north_rows,
    west_cols,
    east_cols,
    sides,
    west_u,
    south_v,
    mix_hi,
    mix_lo,
    land,
    bottom,
    adv_a,
    adv_b,
    hi_a,
    lo_a,
    hi_b,
    lo_b,
    load_sem,
    conc_sem,
    out_sem,
):
    j = lax.axis_index("gy")
    pairs = (
        (land_hbm, land),
        (bottom_hbm, bottom),
        (flow_u_hbm, flow_u),
        (flow_v_hbm, flow_v),
        (west_u_hbm, west_u),
        (south_v_hbm, south_v),
        (west_cols_hbm, west_cols),
        (east_cols_hbm, east_cols),
        (south_rows_hbm, south_rows),
        (north_rows_hbm, north_rows),
        (mix_hi_hbm, mix_hi),
        (mix_lo_hbm, mix_lo),
    )
    loads = [pltpu.make_async_copy(a, b, load_sem.at[n]) for n, (a, b) in enumerate(pairs)]
    for load in loads:
        load.start()
    conc_loads = [
        pltpu.make_async_copy(
            c_hbm.at[:, pl.ds(n * Z_PART, Z_PART)],
            conc.at[:, pl.ds(n * Z_PART, Z_PART), pl.ds(8, Y)],
            conc_sem.at[n],
        )
        for n in range(Z // Z_PART)
    ]
    for load in conc_loads:
        load.start()
    for load in loads:
        load.wait()

    flat = conc.reshape(T * Z * 32, X)
    south_ok = j > 0
    north_ok = j < n_gy - 1

    def put_rows(t, carry):
        place = pl.multiple_of(t * Z, 8)
        base = pl.multiple_of(t * (Z * 32), 8)
        flat[pl.ds(base + 7, Z, stride=32), :] = jnp.where(
            south_ok, south_rows[pl.ds(place, Z), :], 0.0
        )
        flat[pl.ds(base + 8 + Y, Z, stride=32), :] = jnp.where(
            north_ok, north_rows[pl.ds(place, Z), :], 0.0
        )
        return carry

    lax.fori_loop(0, T, put_rows, 0)

    lane = lanes((8, X))
    odd = lane % 2 == 1

    def put_cols(pair, carry):
        place = pl.ds(pl.multiple_of(pair * 8, 8), 8)
        west = west_cols[place, :]
        east = east_cols[place, :]
        first = pl.multiple_of(pair * 16, 8)
        sides[pl.ds(first, 8), :] = jnp.where(odd, roll(west, 1, 1), east)
        sides[pl.ds(first + 8, 8), :] = jnp.where(odd, west, roll(east, -1, 1))
        return carry

    lax.fori_loop(0, Z // 2 + 1, put_cols, 0)

    surface_store = pltpu.make_async_copy(surface_in, surface_hbm, out_sem.at[T // T_PART])
    surface_store.start()

    wide = lanes((Y, X))
    tall = rows((Y, X))
    depth = jnp.where(land[...] > 0, bottom[...], 0).astype(jnp.float32)
    depth_side = sides[pl.ds(Z * 8, 8), :]
    depth_side = jnp.concatenate([roll(depth_side, -1, 1), roll(depth_side, -65, 1)], axis=0)
    depth_east = jnp.where(wide == X - 1, depth_side, roll(depth, -1, 1))
    depth_west = jnp.where(wide == 0, depth_side, roll(depth, 1, 1))
    above = jnp.where(north_ok, north_rows[pl.ds(T * Z, 8), :], 0.0)
    below = jnp.where(south_ok, south_rows[pl.ds(T * Z, 8), :], 0.0)
    depth_north = jnp.where(
        tall == Y - 1, jnp.concatenate([above, above], axis=0), roll(depth, -1, 0)
    )
    depth_south = jnp.where(tall == 0, jnp.concatenate([below, below], axis=0), roll(depth, 1, 0))
    reach_east = jnp.minimum(depth, depth_east)
    reach_west = jnp.minimum(depth, depth_west)
    reach_north = jnp.minimum(depth, depth_north)
    reach_south = jnp.minimum(depth, depth_south)

    def flows(z):
        return flow_u[z], flow_v[z]

    g_above = jnp.zeros((Y, X), jnp.float32)
    r_above = jnp.zeros((Y, X), jnp.float32)
    u, v = flows(0)
    for z in range(Z):
        m, k = z // L, z % L
        u_west = jnp.where(wide == 0, roll(west_u[m], -(4 * k + 1), 1), roll(u, 1, 1))
        row = jnp.where(south_ok, south_v[m, k : k + 1, :], 0.0)
        v_south = jnp.where(tall == 0, jnp.broadcast_to(row, (Y, X)), roll(v, 1, 0))
        ke = jnp.where(reach_east > z, ADVECTION, 0.0)
        kw = jnp.where(reach_west > z, ADVECTION, 0.0)
        kn = jnp.where(reach_north > z, ADVECTION, 0.0)
        ks = jnp.where(reach_south > z, ADVECTION, 0.0)
        coef[z, 0] = (
            1.0
            - ke * jnp.maximum(u, 0.0)
            + kw * jnp.minimum(u_west, 0.0)
            - kn * jnp.maximum(v, 0.0)
            + ks * jnp.minimum(v_south, 0.0)
        )
        coef[z, 1] = -ke * jnp.minimum(u, 0.0)
        coef[z, 2] = kw * jnp.maximum(u_west, 0.0)
        coef[z, 3] = -kn * jnp.minimum(v, 0.0)
        coef[z, 4] = ks * jnp.maximum(v_south, 0.0)
        if z < Z - 1:
            u_next, v_next = flows(z + 1)
            shear = (u - u_next) ** 2 + (v - v_next) ** 2
            rate = KAPPA_BASE + KAPPA_SHEAR * shear / (shear + SHEAR_SCALE)
            g = jnp.where(depth > z + 1, MIXING * rate, 0.0)
            u, v = u_next, v_next
        else:
            g = jnp.zeros((Y, X), jnp.float32)
        inverse = 1.0 / (1.0 + g_above + g - g_above * r_above)
        coef[z, 5] = inverse
        coef[z, 6] = jnp.where(depth > z, ECOLOGY * inverse, 0.0)
        coef[z, 7] = g_above * inverse
        r_above = g * inverse
        coef[z, 8] = r_above
        g_above = g

    def zero_top(t, carry):
        solved[t, 0] = jnp.zeros((Y, X), jnp.float32)
        return carry

    lax.fori_loop(0, T, zero_top, 0)

    def advance(z, adv, hi_ref, lo_ref):
        side = sides[pl.ds(pl.multiple_of(z * 8, 8), 8), :]
        for o in range(2):
            ks = [coef[z, n, 8 * o : 8 * o + 8, :] for n in range(5)]
            for pair in range(T // 2):
                both = []
                for t in (2 * pair, 2 * pair + 1):
                    c = conc[t, z, 8 + 8 * o : 16 + 8 * o, :]
                    edge = roll(side, -(64 * o + 2 * t + 1), 1)
                    east = jnp.where(lane == X - 1, edge, roll(c, -1, 1))
                    west = jnp.where(lane == 0, edge, roll(c, 1, 1))
                    north = conc[t, z, 9 + 8 * o : 17 + 8 * o, :]
                    south = conc[t, z, 7 + 8 * o : 15 + 8 * o, :]
                    a = (ks[0] * c + ks[1] * east) + (
                        ks[2] * west + (ks[3] * north + ks[4] * south)
                    )
                    adv[t, 8 * o : 8 * o + 8, :] = a
                    both.append(jnp.tanh(a))
                y = jnp.concatenate(both, axis=0)
                hi = y.astype(jnp.bfloat16)
                lo = (y - hi.astype(jnp.float32)).astype(jnp.bfloat16)
                hi_ref[16 * pair : 16 * pair + 16, o * X : o * X + X] = hi
                lo_ref[16 * pair : 16 * pair + 16, o * X : o * X + X] = lo

    def mix(hi_ref, lo_ref):
        return (
            jnp.dot(mix_hi[...], hi_ref[...], preferred_element_type=jnp.float32)
            + jnp.dot(mix_lo[...], hi_ref[...], preferred_element_type=jnp.float32)
            + jnp.dot(mix_hi[...], lo_ref[...], preferred_element_type=jnp.float32)
        )

    def finish(z, adv, source):
        for o in range(2):
            ks = [coef[z, n, 8 * o : 8 * o + 8, :] for n in range(5, 8)]
            for t in range(T):
                s = source[8 * t : 8 * t + 8, o * X : o * X + X]
                solved[t, z + 1, 8 * o : 8 * o + 8, :] = (
                    ks[0] * adv[t, 8 * o : 8 * o + 8, :]
                    + ks[1] * s
                    + ks[2] * solved[t, z, 8 * o : 8 * o + 8, :]
                )

    def two(i, carry):
        z = 2 * i

        source = mix(hi_a, lo_a)
        advance(z + 1, adv_b, hi_b, lo_b)
        finish(z, adv_a, source)
        source = mix(hi_b, lo_b)
        advance(z + 2, adv_a, hi_a, lo_a)
        finish(z + 1, adv_b, source)
        return carry

    for load in conc_loads:
        load.wait()
    advance(0, adv_a, hi_a, lo_a)
    lax.fori_loop(0, Z // 2 - 1, two, 0)
    source = mix(hi_a, lo_a)
    advance(Z - 1, adv_b, hi_b, lo_b)
    finish(Z - 2, adv_a, source)
    finish(Z - 1, adv_b, mix(hi_b, lo_b))

    def store(n):
        return pltpu.make_async_copy(
            solved.at[pl.ds(n * T_PART, T_PART), pl.ds(1, Z)],
            out_hbm.at[pl.ds(n * T_PART, T_PART)],
            out_sem.at[n],
        )

    def back(n, carry):
        base = n * T_PART
        x = [solved[base + t, Z] for t in range(T_PART)]
        for z in range(Z - 2, -1, -1):
            r = coef[z, 8]
            for t in range(T_PART):
                x[t] = solved[base + t, z + 1] + r * x[t]
                solved[base + t, z + 1] = x[t]
        store(n).start()
        return carry

    lax.fori_loop(0, T // T_PART, back, 0)
    for n in range(T // T_PART):
        store(n).wait()
    surface_store.wait()


def columns(n_gy, conc, parts, land, bottom):
    f32 = jnp.float32
    dma = pltpu.SemaphoreType.DMA
    mix_type = pltpu.VMEM((8 * T, 2 * X), jnp.bfloat16)
    return pl.pallas_call(
        functools.partial(column_kernel, n_gy),
        out_shape=(
            jax.ShapeDtypeStruct((T, Z, Y, X), f32),
            jax.ShapeDtypeStruct((FOLDED, X), f32),
        ),
        in_specs=[HBM] * 14,
        out_specs=(HBM, HBM),
        scratch_shapes=[
            pltpu.VMEM((T, Z, 32, X), f32),
            pltpu.VMEM((T, Z + 1, Y, X), f32),
            pltpu.VMEM((Z, COEF, Y, X), f32),
            pltpu.VMEM((Z, Y, X), f32),
            pltpu.VMEM((Z, Y, X), f32),
            pltpu.VMEM((EDGE_ROWS, X), f32),
            pltpu.VMEM((EDGE_ROWS, X), f32),
            pltpu.VMEM((EDGE_COLS, X), f32),
            pltpu.VMEM((EDGE_COLS, X), f32),
            pltpu.VMEM((2 * EDGE_COLS, X), f32),
            pltpu.VMEM((G, Y, X), f32),
            pltpu.VMEM((G, 8, X), f32),
            pltpu.VMEM((8 * T, 8 * T), jnp.bfloat16),
            pltpu.VMEM((8 * T, 8 * T), jnp.bfloat16),
            pltpu.VMEM((Y, X), jnp.int32),
            pltpu.VMEM((Y, X), jnp.int32),
            pltpu.VMEM((T, Y, X), f32),
            pltpu.VMEM((T, Y, X), f32),
            mix_type,
            mix_type,
            mix_type,
            mix_type,
            dma((12,)),
            dma((Z // Z_PART,)),
            dma((T // T_PART + 1,)),
        ],
        compiler_params=pltpu.CompilerParams(vmem_limit_bytes=60 * 1024 * 1024),
        name="columns",
    )(conc, *parts, land, bottom)


def shards(east_velocity, north_velocity, sea_surface, tracers, land_sea, bottom_level, coupling):
    n_gy = lax.axis_size("gy")
    n_gx = lax.axis_size("gx")
    eta = sea_surface.reshape(FOLDED, X)
    parts = exchange(
        n_gy,
        n_gx,
        east_velocity.reshape(L, FOLDED, X),
        north_velocity.reshape(L, FOLDED, X),
        eta,
        tracers.reshape(T * Z * Y, X),
        land_sea,
        bottom_level,
        coupling,
    )
    tracers_next, surface_next = columns(n_gy, tracers, parts, land_sea, bottom_level)
    return tracers_next, surface_next.reshape(Y, G, X)


def solution(mesh):
    placed = (
        P("group", "gy", None, "gx"),
        P("group", "gy", None, "gx"),
        P("gy", None, "gx"),
        P(None, None, "gy", ("group", "gx")),
        P("gy", ("group", "gx")),
        P("gy", ("group", "gx")),
        P(),
    )
    return jax.shard_map(
        shards,
        mesh=mesh,
        in_specs=placed,
        out_specs=(P(None, None, "gy", ("group", "gx")), P("gy", None, "gx")),
        check_vma=False,
    )
```
